32 devices in a mesh: fsdp: 16 (over z, y, x), ctx: 2 (over core).
Axes of the slice: x: 2, y: 2, z: 4, core: 2. Of those that a mesh axis runs over, the one named last changes fastest.
Arguments:
- tokens: bfloat16 [16, 2, 512, 768], P('fsdp', 'ctx'), may hold values from -6 to 6
- pair_order: int32 [16, 2], P('fsdp'), may hold values from 0 to 1, each once within a row
- gain_one: bfloat16 [768], P('fsdp'), may hold values from 0.5 to 1.5
- bias_one: bfloat16 [768], P('fsdp'), may hold values from -3 to 3
- w_qkv: bfloat16 [768, 2304], P('fsdp'), may hold values from -0.21875 to 0.21875
- bias_q: bfloat16 [768], P('fsdp'), may hold values from -3 to 3
- bias_v: bfloat16 [768], P('fsdp'), may hold values from -3 to 3
- w_out: bfloat16 [768, 768], P('fsdp'), may hold values from -0.875 to 0.875
- bias_out: bfloat16 [768], P('fsdp'), may hold values from -3 to 3
- gain_two: bfloat16 [768], P('fsdp'), may hold values from 0.5 to 1.5
- bias_two: bfloat16 [768], P('fsdp'), may hold values from -3 to 3
- w_fc: bfloat16 [768, 3072], P('fsdp'), may hold values from -0.21875 to 0.21875
- bias_fc: bfloat16 [3072], P('fsdp'), may hold values from -3 to 3
- w_proj: bfloat16 [3072, 768], P('fsdp'), may hold values from -0.109375 to 0.109375
- bias_proj: bfloat16 [768], P('fsdp'), may hold values from -3 to 3
- cotangent: bfloat16 [16, 2, 512, 768], P('fsdp', 'ctx'), may hold values from -6 to 6
Outputs:
- layer_out: bfloat16 [16, 2, 512, 768], P('fsdp', 'ctx')
- grad_tokens: float32 [16, 2, 512, 768], P('fsdp', 'ctx')
- grad_gain_one: float32 [768], P(('fsdp', 'ctx'))
- grad_bias_one: float32 [768], P(('fsdp', 'ctx'))
- grad_w_qkv: float32 [768, 2304], P(('fsdp', 'ctx'))
- grad_bias_q: float32 [768], P(('fsdp', 'ctx'))
- grad_bias_v: float32 [768], P(('fsdp', 'ctx'))
- grad_w_out: float32 [768, 768], P(('fsdp', 'ctx'))
- grad_bias_out: float32 [768], P(('fsdp', 'ctx'))
- grad_gain_two: float32 [768], P(('fsdp', 'ctx'))
- grad_bias_two: float32 [768], P(('fsdp', 'ctx'))
- grad_w_fc: float32 [768, 3072], P(('fsdp', 'ctx'))
- grad_bias_fc: float32 [3072], P(('fsdp', 'ctx'))
- grad_w_proj: float32 [3072, 768], P(('fsdp', 'ctx'))
- grad_bias_proj: float32 [768], P(('fsdp', 'ctx'))
The draws below stay inside these ranges and needn't reach their ends.
Inputs may be any that keep to these rules, and one draw needn't show every extreme that they name: `pair_order`: each row is a permutation of 0 to 1.
All inputs are finite; a program needn't handle non-finite values.
Results may differ from the reference program's by a relative error of at most 0.013.
Values may be sent and summed in bfloat16 or wider, within the bound.
No kernel may reach another device: no remote copies, remote signals or barrier semaphores. Data moves between devices by JAX's collectives and lax.ppermute only.
A program may use at most 192 MiB of HBM per device.

```python
import jax
import jax.numpy as jnp
from jax import lax

D = 768
HEADS = 12
HEAD_DIM = 64
FF = 3072
BLK = 256
SEQUENCES = 16
N_CTX = 2


def shard_levels(key, dims, pieces, least, top_value):
    def one(axis_at, blocks):
        heights = jax.random.uniform(jax.random.fold_in(jax.random.fold_in(key, 6), axis_at), (blocks,), jnp.float32, least / len(pieces), top_value / len(pieces))
        return jnp.repeat(jnp.exp(heights), dims[axis_at] // blocks).reshape((-1,) + (1,) * (len(dims) - axis_at - 1))

    gain = one(*pieces[0])
    for cut in pieces[1:]:
        gain = gain * one(*cut)
    return gain


def normal_values(own_key, dims, scale, bound, shards=(), held_as=jnp.bfloat16):
    entries = jax.random.normal(own_key, dims, jnp.float32) * scale
    if len(shards) > 0:
        entries = shard_levels(own_key, dims, shards, -0.22, 0.18) * entries
    return jnp.clip(entries, min=-bound, max=bound).astype(held_as)


def setup_inputs(seed: int = 0) -> dict:
    keys = jax.random.split(jax.random.key(seed), 17)
    tokens = normal_values(keys[0], (SEQUENCES, N_CTX, 2 * BLK, D), 1.0, 6.0, ((0, 16), (1, 2)))
    pair_order = jax.vmap(lambda own: jax.random.permutation(own, N_CTX))(jax.random.split(keys[1], SEQUENCES)).reshape((SEQUENCES, N_CTX)).astype(jnp.int32)
    gain_one = jnp.clip(1.0 + 0.1 * jax.random.normal(keys[2], (D,), jnp.float32), 0.5, 1.5).astype(jnp.bfloat16)
    bias_one = normal_values(keys[3], (D,), 0.5, 3.0, ((0, 16),))
    w_qkv = normal_values(keys[4], (D, 3 * D), D ** -0.5, 0.21875, ((0, 16),))
    bias_q = normal_values(keys[5], (D,), 0.5, 3.0, ((0, 16),))
    bias_v = normal_values(keys[6], (D,), 0.5, 3.0, ((0, 16),))
    w_out = normal_values(keys[7], (D, D), (D // 16) ** -0.5, 0.875, ((0, 16),))
    bias_out = normal_values(keys[8], (D,), 0.5, 3.0, ((0, 16),))
    gain_two = jnp.clip(1.0 + 0.1 * jax.random.normal(keys[9], (D,), jnp.float32), 0.5, 1.5).astype(jnp.bfloat16)
    bias_two = normal_values(keys[10], (D,), 0.5, 3.0, ((0, 16),))
    w_fc = normal_values(keys[11], (D, FF), D ** -0.5, 0.21875, ((0, 16),))
    bias_fc = normal_values(keys[12], (FF,), 0.5, 3.0, ((0, 16),))
    w_proj = normal_values(keys[13], (FF, D), FF ** -0.5, 0.109375, ((0, 16),))
    bias_proj = normal_values(keys[14], (D,), 0.5, 3.0, ((0, 16),))
    cotangent = normal_values(keys[15], (SEQUENCES, N_CTX, 2 * BLK, D), 1.0, 6.0, ((0, 16), (1, 2)))
    return dict(tokens=tokens, pair_order=pair_order, gain_one=gain_one, bias_one=bias_one, w_qkv=w_qkv, bias_q=bias_q, bias_v=bias_v, w_out=w_out, bias_out=bias_out, gain_two=gain_two, bias_two=bias_two, w_fc=w_fc, bias_fc=bias_fc, w_proj=w_proj, bias_proj=bias_proj, cotangent=cotangent)


@jax.custom_vjp
def low(v):
    return lax.optimization_barrier(v.astype(jnp.bfloat16)).astype(jnp.float32)

@jax.custom_vjp
def low_back(v):
    return v

def low_keep(v):
    return (low(v), None)

def low_pass(kept, grad):
    return (grad,)

def back_keep(v):
    return (v, None)

def back_low(kept, grad):
    return (low(grad),)
low.defvjp(low_keep, low_pass)
low_back.defvjp(back_keep, back_low)
EPSILON = 1e-05
NEG_FILL = -1e+30
PRECISE = lax.Precision.HIGHEST

def matmul_hi(left, right):
    return jnp.dot(left, right, precision=PRECISE, preferred_element_type=jnp.float32)

def layer_norm(values, norm_gain, norm_bias):
    average = lax.optimization_barrier(jnp.mean(values, axis=-1, keepdims=True))
    centred = values - average
    variance = lax.optimization_barrier(jnp.mean(centred * centred, axis=-1, keepdims=True))
    return centred * lax.rsqrt(variance + EPSILON) * norm_gain + norm_bias

def block_places(pair_order):
    starts = jnp.stack([pair_order, 2 * N_CTX - 1 - pair_order], axis=-1) * BLK
    offsets = jnp.arange(BLK, dtype=jnp.int32)
    return (starts[..., None] + offsets).reshape(pair_order.shape[0], N_CTX * 2 * BLK).astype(jnp.int32)

def sequence_forward(inputs, places, params):
    gain_one, bias_one, w_qkv, bias_q, bias_v, w_out, bias_out, gain_two, bias_two, w_fc, bias_fc, w_proj, bias_proj = params
    length = inputs.shape[0]
    normed = low(layer_norm(inputs, gain_one, bias_one))
    project = matmul_hi(normed, w_qkv)
    queries = low(low_back(project[:, :D] + bias_q)).reshape(length, HEADS, HEAD_DIM)
    keys_seq = low(low_back(project[:, D:2 * D])).reshape(length, HEADS, HEAD_DIM)
    values_seq = low(low_back(project[:, 2 * D:] + bias_v)).reshape(length, HEADS, HEAD_DIM)
    scores = jnp.einsum('qhd,khd->hqk', queries, keys_seq, precision=PRECISE) * HEAD_DIM ** (-0.5)
    scores = low_back(scores)
    allowed = places[None, :, None] >= places[None, None, :]
    scores = jnp.where(allowed, scores, NEG_FILL)
    row_top = lax.optimization_barrier(jnp.max(scores, axis=-1, keepdims=True))
    exponent = jnp.exp(scores - row_top)
    chances = low(exponent / lax.optimization_barrier(jnp.sum(exponent, axis=-1, keepdims=True)))
    mixed = jnp.einsum('hqk,khd->qhd', chances, values_seq, precision=PRECISE).reshape(length, D)
    mixed = low(low_back(mixed))
    branch = low_back(matmul_hi(mixed, w_out) + bias_out)
    middle = inputs + branch
    normed_two = low(layer_norm(middle, gain_two, bias_two))
    hidden_pre = low_back(matmul_hi(normed_two, w_fc) + bias_fc)
    active = low(jax.nn.gelu(hidden_pre, approximate=True))
    return middle + matmul_hi(active, w_proj) + bias_proj

def reference(tokens, pair_order, gain_one, bias_one, w_qkv, bias_q, bias_v, w_out, bias_out, gain_two, bias_two, w_fc, bias_fc, w_proj, bias_proj, cotangent):
    params = tuple((member.astype(jnp.float32) for member in (gain_one, bias_one, w_qkv, bias_q, bias_v, w_out, bias_out, gain_two, bias_two, w_fc, bias_fc, w_proj, bias_proj)))
    places = block_places(pair_order)
    inputs = tokens.astype(jnp.float32).reshape(SEQUENCES, N_CTX * 2 * BLK, D)
    forward_one = jax.checkpoint(sequence_forward)

    def forward(inputs_all, params_all):

        def forward_member(member):
            return forward_one(member[0], member[1], params_all)
        return lax.map(forward_member, (inputs_all, places))
    outputs, pullback = jax.vjp(forward, inputs, params)
    grad_inputs, grad_params = pullback(cotangent.astype(jnp.float32).reshape(inputs.shape))
    grad_gain_one, grad_bias_one, grad_w_qkv, grad_bias_q, grad_bias_v, grad_w_out, grad_bias_out, grad_gain_two, grad_bias_two, grad_w_fc, grad_bias_fc, grad_w_proj, grad_bias_proj = grad_params
    return (outputs.astype(jnp.bfloat16).reshape(tokens.shape), grad_inputs.reshape(tokens.shape), grad_gain_one, grad_bias_one, grad_w_qkv, grad_bias_q, grad_bias_v, grad_w_out, grad_bias_out, grad_gain_two, grad_bias_two, grad_w_fc, grad_bias_fc, grad_w_proj, grad_bias_proj)
```

```python
import functools

import jax
import jax.numpy as jnp
from jax import lax
from jax.experimental import pallas as pl
from jax.experimental.pallas import tpu as pltpu
from jax.sharding import PartitionSpec as P

HEADS = 12
HEAD_DIM = 64


EPSILON = 1e-05
NEG_FILL = -1e30


def layer_norm(values, norm_gain, norm_bias):
    average = jnp.mean(values, axis=-1, keepdims=True)
    centred = values - average
    variance = jnp.mean(centred * centred, axis=-1, keepdims=True)
    return centred * lax.rsqrt(variance + EPSILON) * norm_gain + norm_bias


def gelu_tanh(values):
    return jax.nn.gelu(values, approximate=True)


def block_places(pair_order, block_len):
    count = pair_order.shape[1]
    starts = jnp.stack([pair_order, 2 * count - 1 - pair_order], axis=2) * block_len
    offsets = jnp.arange(block_len, dtype=jnp.int32)
    placed = starts[:, :, :, None] + offsets
    return placed.reshape(pair_order.shape[0], count * 2 * block_len)


def to_heads(array):
    split = array.reshape(array.shape[0], array.shape[1], HEADS, HEAD_DIM)
    return jnp.moveaxis(split, 2, 0)


def from_heads(array):
    moved = jnp.moveaxis(array, 0, 2)
    return moved.reshape(moved.shape[0], moved.shape[1], HEADS * HEAD_DIM)


def inner_rows(left, right):
    return lax.dot_general(
        left, right, (((0,), (0,)), ((), ())), preferred_element_type=jnp.float32
    )


def times_t(left, right):
    return lax.dot_general(
        left, right, (((1,), (1,)), ((), ())), preferred_element_type=jnp.float32
    )

ROWS = 48
LANES = 128
VMEM_BYTES = 48 * 1024 * 1024


def bits_of(count):
    return count.bit_length() - 1


def swap_chip(value, count, bit):
    return lax.ppermute(value, "fsdp", [(i, i ^ (1 << bit)) for i in range(count)])


def swap_core(value, count):
    return lax.ppermute(value, "ctx", [(i, i ^ 1) for i in range(count)])


def stage_orders(count):
    nbits = bits_of(count)
    high = list(range(nbits - 1, 1, -1))
    return high, high + [0, 1], high + [1, 0]


def mask_of(place, order):
    return sum(((place >> k) & 1) << bit for k, bit in enumerate(order))


def gather_pieces(shard, width_a, fsdp, n_ctx, core):
    half = shard.shape[-1] // 2
    high, order_a, order_b = stage_orders(fsdp)
    held = lax.dynamic_slice_in_dim(shard, core * half, half, 2)
    for bit in high:
        held = jnp.concatenate([held, swap_chip(held, fsdp, bit)], axis=0)
    part_a, part_b = held[..., :width_a], held[..., width_a:]
    part_a = jnp.concatenate([part_a, swap_chip(part_a, fsdp, order_a[-2])], axis=0)
    part_b = jnp.concatenate([part_b, swap_chip(part_b, fsdp, order_b[-2])], axis=0)
    last_a = swap_chip(part_a, fsdp, order_a[-1])
    last_b = swap_chip(part_b, fsdp, order_b[-1])
    own = (part_a, last_a, part_b, last_b)
    return own + tuple(swap_core(member, n_ctx) for member in own)


def piece_moves(fsdp, half, width_a):
    high, order_a, order_b = stage_orders(fsdp)
    moves = []
    for other in (0, 1):
        for order, start, width in ((order_a, 0, width_a), (order_b, width_a, half - width_a)):
            for first in (0, fsdp // 2):
                moves.append((order, first, other, start, width))
    return moves


def assemble_kernel(fsdp, half, width_a, rows, column_blocks, index_ref, *refs):
    pieces, whole = refs[:8], refs[8]
    chip, core = index_ref[0], index_ref[1]
    model = whole.shape[1]
    for number, (order, first, other, start, width) in enumerate(piece_moves(fsdp, half, width_a)):
        side = (1 - core) if other else core
        column = side * half + start
        for place in range(fsdp // 2):
            origin = chip ^ mask_of(first + place, order)
            if column_blocks == 1:
                row, lane = origin * rows, pl.multiple_of(column, LANES)
            else:
                row, lane = (origin * column_blocks + column // model) * rows, 0
            whole[pl.ds(pl.multiple_of(row, 16), rows), pl.ds(lane, width)] = pieces[number][place]


def assemble(pieces, where, width_a, fsdp, column_blocks, model):
    rows = pieces[0].shape[1]
    half = width_a + pieces[2].shape[2]
    shape = (fsdp * rows, 2 * half) if column_blocks == 1 else (fsdp * rows * column_blocks, model)
    return pl.pallas_call(
        functools.partial(assemble_kernel, fsdp, half, width_a, rows, column_blocks),
        out_shape=jax.ShapeDtypeStruct(shape, pieces[0].dtype),
        in_specs=[pl.BlockSpec(memory_space=pltpu.SMEM)] + [pl.BlockSpec(memory_space=pltpu.VMEM)] * 8,
        out_specs=pl.BlockSpec(memory_space=pltpu.VMEM),
        compiler_params=pltpu.CompilerParams(vmem_limit_bytes=VMEM_BYTES),
    )(where, *pieces)


def cut_kernel(fsdp, half, width_a, rows, column_blocks, index_ref, whole, *pieces):
    chip, core = index_ref[0], index_ref[1]
    high, order_a, order_b = stage_orders(fsdp)
    model = whole.shape[1]
    for number, (other, order, start, width) in enumerate(
        (
            (0, order_a, 0, width_a),
            (0, order_b, width_a, half - width_a),
            (1, order_a, 0, width_a),
            (1, order_b, width_a, half - width_a),
        )
    ):
        side = (1 - core) if other else core
        column = side * half + start
        for place in range(fsdp):
            origin = chip ^ mask_of(place, order)
            if column_blocks == 1:
                row, lane = origin * rows, pl.multiple_of(column, LANES)
            else:
                row, lane = (origin * column_blocks + column // model) * rows, 0
            block = whole[pl.ds(pl.multiple_of(row, 8), rows), pl.ds(lane, width)]
            pieces[number][place] = block.astype(pieces[number].dtype)


def cut(whole, where, rows, half, width_a, fsdp, column_blocks):
    shapes = [(fsdp, rows, width_a), (fsdp, rows, half - width_a)] * 2
    return pl.pallas_call(
        functools.partial(cut_kernel, fsdp, half, width_a, rows, column_blocks),
        out_shape=[jax.ShapeDtypeStruct(shape, jnp.bfloat16) for shape in shapes],
        in_specs=[pl.BlockSpec(memory_space=pltpu.SMEM), pl.BlockSpec(memory_space=pltpu.VMEM)],
        out_specs=[pl.BlockSpec(memory_space=pltpu.VMEM)] * 4,
        compiler_params=pltpu.CompilerParams(vmem_limit_bytes=VMEM_BYTES),
    )(where, whole)


def add(left, right):
    return left.astype(jnp.float32) + right.astype(jnp.float32)


def scatter_pieces(pieces, fsdp, n_ctx):
    keep_a, keep_b, send_a, send_b = pieces
    high, order_a, order_b = stage_orders(fsdp)
    low = jnp.bfloat16
    sum_a = add(keep_a, swap_core(send_a, n_ctx)).astype(low)
    sum_b = add(keep_b, swap_core(send_b, n_ctx)).astype(low)
    for step in (-1, -2):
        middle = sum_a.shape[0] // 2
        got_a = swap_chip(sum_a[middle:], fsdp, order_a[step])
        got_b = swap_chip(sum_b[middle:], fsdp, order_b[step])
        sum_a = add(sum_a[:middle], got_a).astype(low)
        sum_b = add(sum_b[:middle], got_b).astype(low)
    total = jnp.concatenate([sum_a, sum_b], axis=2)
    for bit in reversed(high):
        middle = total.shape[0] // 2
        got = swap_chip(total[middle:], fsdp, bit)
        kept = total[:middle]
        total = add(kept, got)
        if middle > 1:
            total = total.astype(low)
    total = total[0]
    if n_ctx > 2:
        groups = [list(range(0, n_ctx, 2)), list(range(1, n_ctx, 2))]
        total = lax.psum(total, "ctx", axis_index_groups=groups)
    return total


def share_rows(total, n_ctx, ctx_index):
    rows = total.shape[0] // n_ctx
    mine = lax.dynamic_slice_in_dim(total, ctx_index * rows, rows, 0)
    theirs = swap_core(lax.dynamic_slice_in_dim(total, (ctx_index ^ 1) * rows, rows, 0), n_ctx)
    first = (ctx_index & 1) == 0
    return jnp.concatenate([jnp.where(first, mine, theirs), jnp.where(first, theirs, mine)], axis=1)


def share_blocks(total, n_ctx, ctx_index, blocks):
    rows = total.shape[0]
    if n_ctx > 2:
        theirs = swap_core(total, n_ctx)
        first = (ctx_index & 1) == 0
        total = jnp.concatenate([jnp.where(first, total, theirs), jnp.where(first, theirs, total)], axis=1)
    parts = blocks if n_ctx > 2 else blocks // 2
    stacked = jnp.moveaxis(total.reshape(rows, parts, -1), 1, 0).reshape(parts * rows, -1)
    if n_ctx > 2:
        count = stacked.shape[0] // n_ctx
        stacked = lax.dynamic_slice_in_dim(stacked, ctx_index * count, count, 0)
    return stacked


def body(
    tokens,
    pair_order,
    gain_one,
    bias_one,
    w_qkv,
    bias_q,
    bias_v,
    w_out,
    bias_out,
    gain_two,
    bias_two,
    w_fc,
    bias_fc,
    w_proj,
    bias_proj,
    cotangent,
):
    seq_count, unused, length, model_width = tokens.shape
    block_len = length // 2
    ctx_index = lax.axis_index("ctx")
    score_scale = HEAD_DIM ** (-0.5)
    fsdp = lax.axis_size("fsdp")
    n_ctx = lax.axis_size("ctx")
    core = ctx_index & 1
    where = jnp.stack([lax.axis_index("fsdp"), core]).astype(jnp.int32)
    rows = gain_one.shape[0]
    small_rows = jnp.concatenate(
        [
            jnp.stack(
                [gain_one, bias_one, bias_q, bias_v, bias_out, gain_two, bias_two, bias_proj], axis=1
            ),
            bias_fc.reshape(-1, rows).T,
        ],
        axis=1,
    )
    small_count = small_rows.shape[1]
    small_rows = jnp.pad(small_rows, ((0, 0), (0, 2 * LANES - small_count)))
    width_one, width_two, width_three = 640, 1024, 768
    model_full = fsdp * rows
    blocks = w_proj.shape[0] // rows
    group_one = jnp.concatenate([w_qkv, small_rows], axis=1)[None]
    group_two = jnp.concatenate([w_fc, w_out], axis=1)[None]
    group_three = jnp.moveaxis(w_proj.reshape(blocks, rows, model_full), 0, 1).reshape(1, rows, -1)
    whole_one = assemble(
        gather_pieces(group_one, width_one, fsdp, n_ctx, core), where, width_one, fsdp, 1, model_full
    )
    whole_two = assemble(
        gather_pieces(group_two, width_two, fsdp, n_ctx, core), where, width_two, fsdp, 1, model_full
    )
    proj_full = assemble(
        gather_pieces(group_three, width_three, fsdp, n_ctx, core), where, width_three, fsdp, blocks, model_full
    )
    qkv_full = whole_one[:, : 3 * model_full]
    fc_full = whole_two[:, : w_fc.shape[1]]
    out_full = whole_two[:, w_fc.shape[1] :]
    small_full = whole_one[:, 3 * model_full : 3 * model_full + small_count].T.astype(jnp.float32)
    (
        gain_first,
        bias_first,
        query_bias,
        value_bias,
        out_bias,
        gain_second,
        bias_second,
        proj_bias,
    ) = [small_full[i] for i in range(8)]
    fc_bias = jnp.moveaxis(small_full[8:].reshape(blocks, fsdp, rows), 0, 1).reshape(-1)
    flat_rows = tokens.astype(jnp.float32).reshape(seq_count * length, model_width)
    norm_first, pull_first = jax.vjp(layer_norm, flat_rows, gain_first, bias_first)
    normed = norm_first.astype(jnp.bfloat16)
    project = jnp.dot(normed, qkv_full, preferred_element_type=jnp.float32)
    queries = (
        (project[:, :model_width] + query_bias)
        .astype(jnp.bfloat16)
        .reshape(seq_count, length, model_width)
    )
    keys_own = (
        project[:, model_width : 2 * model_width]
        .astype(jnp.bfloat16)
        .reshape(seq_count, length, model_width)
    )
    values_own = (
        (project[:, 2 * model_width :] + value_bias)
        .astype(jnp.bfloat16)
        .reshape(seq_count, length, model_width)
    )
    keys_all, values_all = (
        lax.all_gather(keys_own, "ctx", axis=1, tiled=True),
        lax.all_gather(values_own, "ctx", axis=1, tiled=True),
    )
    all_places = block_places(pair_order, block_len)
    own_places = lax.dynamic_slice_in_dim(all_places, ctx_index * length, length, 1)
    allowed = own_places[:, :, None] >= all_places[:, None, :]
    query_heads = to_heads(queries)
    key_heads = to_heads(keys_all)
    value_heads = to_heads(values_all)

    def head_forward(member):
        query_h, key_h, value_h = member
        scores = (
            jnp.einsum("sqd,skd->sqk", query_h, key_h, preferred_element_type=jnp.float32)
            * score_scale
        )
        scores = jnp.where(allowed, scores, NEG_FILL)
        row_top = jnp.max(scores, axis=-1, keepdims=True)
        exponent = jnp.exp(scores - row_top)
        row_sum = jnp.sum(exponent, axis=-1, keepdims=True)
        chances = (exponent / row_sum).astype(jnp.bfloat16)
        output = jnp.einsum("sqk,skd->sqd", chances, value_h, preferred_element_type=jnp.float32)
        return (output, (row_top + jnp.log(row_sum))[..., 0])

    head_out, log_total = lax.map(head_forward, (query_heads, key_heads, value_heads))
    mixed = from_heads(head_out).astype(jnp.bfloat16).reshape(seq_count * length, model_width)
    branch = jnp.dot(mixed, out_full, preferred_element_type=jnp.float32) + out_bias
    middle = flat_rows + branch
    norm_second, pull_second = jax.vjp(layer_norm, middle, gain_second, bias_second)
    normed_two = norm_second.astype(jnp.bfloat16)
    hidden_pre = jnp.dot(normed_two, fc_full, preferred_element_type=jnp.float32) + fc_bias
    active_full, pull_gelu = jax.vjp(gelu_tanh, hidden_pre)
    active = active_full.astype(jnp.bfloat16)
    result_rows = (
        middle + jnp.dot(active, proj_full, preferred_element_type=jnp.float32) + proj_bias
    )
    out_tokens = result_rows.astype(jnp.bfloat16).reshape(tokens.shape)
    grad_rows = cotangent.reshape(seq_count * length, model_width)
    grad_float = grad_rows.astype(jnp.float32)
    grad_proj = inner_rows(active, grad_rows)
    sum_proj_bias = jnp.sum(grad_float, axis=0)
    d_active = times_t(grad_rows, proj_full)
    d_pre = pull_gelu(d_active)[0].astype(jnp.bfloat16)
    grad_fc = inner_rows(normed_two, d_pre)
    sum_fc_bias = jnp.sum(d_pre.astype(jnp.float32), axis=0)
    d_normed_two = times_t(d_pre, fc_full)
    d_middle_norm, grad_gain_second, grad_bias_second = pull_second(d_normed_two)
    d_middle = grad_float + d_middle_norm
    d_branch = d_middle.astype(jnp.bfloat16)
    grad_out_w = inner_rows(mixed, d_branch)
    sum_out_bias = jnp.sum(d_branch.astype(jnp.float32), axis=0)
    d_mixed = (
        times_t(d_branch, out_full).astype(jnp.bfloat16).reshape(seq_count, length, model_width)
    )
    dmix_heads = to_heads(d_mixed)

    def score_grads(query_h, key_h, value_h, dmix_h, lse_h, mask):
        scores = (
            jnp.einsum("sqd,skd->sqk", query_h, key_h, preferred_element_type=jnp.float32)
            * score_scale
        )
        prob_full = jnp.exp(jnp.where(mask, scores, NEG_FILL) - lse_h[..., None])
        d_probs = jnp.einsum("sqd,skd->sqk", dmix_h, value_h, preferred_element_type=jnp.float32)
        delta = jnp.sum(prob_full * d_probs, axis=-1)
        return (prob_full, d_probs, delta)

    def head_back_keys(member):
        query_h, key_h, value_h, dmix_h, lse_h = member
        prob_full, d_probs, delta = score_grads(query_h, key_h, value_h, dmix_h, lse_h, allowed)
        d_scores = (prob_full * (d_probs - delta[..., None])).astype(jnp.bfloat16)
        d_query = (
            jnp.einsum("sqk,skd->sqd", d_scores, key_h, preferred_element_type=jnp.float32)
            * score_scale
        )
        d_key = (
            jnp.einsum("sqk,sqd->skd", d_scores, query_h, preferred_element_type=jnp.float32)
            * score_scale
        )
        d_value = jnp.einsum(
            "sqk,sqd->skd",
            prob_full.astype(jnp.bfloat16),
            dmix_h,
            preferred_element_type=jnp.float32,
        )
        return (d_query, d_key, d_value)

    dq_heads, dk_heads, dv_heads = lax.map(
        head_back_keys, (query_heads, key_heads, value_heads, dmix_heads, log_total)
    )
    d_key_own, d_value_own = (
        lax.psum_scatter(
            from_heads(dk_heads).astype(jnp.bfloat16), "ctx", scatter_dimension=1, tiled=True
        ).astype(jnp.float32),
        lax.psum_scatter(
            from_heads(dv_heads).astype(jnp.bfloat16), "ctx", scatter_dimension=1, tiled=True
        ).astype(jnp.float32),
    )
    d_query_all = from_heads(dq_heads).astype(jnp.bfloat16)
    d_key_round = d_key_own.astype(jnp.bfloat16)
    d_value_round = d_value_own.astype(jnp.bfloat16)
    d_qkv = jnp.concatenate([d_query_all, d_key_round, d_value_round], axis=-1).reshape(
        seq_count * length, 3 * model_width
    )
    grad_qkv = inner_rows(normed, d_qkv)
    sum_query_bias = jnp.sum(d_query_all.astype(jnp.float32), axis=(0, 1))
    sum_value_bias = jnp.sum(d_value_round.astype(jnp.float32), axis=(0, 1))
    d_normed = times_t(d_qkv, qkv_full)
    d_rows_norm, grad_gain_first, grad_bias_first = pull_first(d_normed)
    grad_inputs = (d_middle + d_rows_norm).reshape(tokens.shape)
    low = jnp.bfloat16
    sums_fc = jnp.moveaxis(sum_fc_bias.reshape(fsdp, n_ctx, blocks, rows // n_ctx), 2, 0).reshape(blocks, -1)
    small_sums = jnp.concatenate(
        [
            jnp.stack(
                [
                    grad_gain_first,
                    grad_bias_first,
                    sum_query_bias,
                    sum_value_bias,
                    sum_out_bias,
                    grad_gain_second,
                    grad_bias_second,
                    sum_proj_bias,
                ]
            ),
            sums_fc,
        ]
    )
    small_sums = jnp.pad(small_sums, ((0, 2 * LANES - small_count), (0, 0))).T
    grads_one = jnp.concatenate([grad_qkv.astype(low), small_sums.astype(low)], axis=1)
    grads_two = jnp.concatenate([grad_fc.astype(low), grad_out_w.astype(low)], axis=1)
    parts_three = cut(grad_proj.astype(low), where, rows, blocks * model_full // 2, width_three, fsdp, blocks)
    parts_two = cut(grads_two, where, rows, grads_two.shape[1] // 2, width_two, fsdp, 1)
    parts_one = cut(grads_one, where, rows, grads_one.shape[1] // 2, width_one, fsdp, 1)
    share_proj = share_blocks(scatter_pieces(parts_three, fsdp, n_ctx), n_ctx, ctx_index, blocks)
    share_two = share_rows(scatter_pieces(parts_two, fsdp, n_ctx), n_ctx, ctx_index)
    share_one = share_rows(scatter_pieces(parts_one, fsdp, n_ctx), n_ctx, ctx_index)
    share_qkv = share_one[:, : 3 * model_width]
    share_fc = share_two[:, : w_fc.shape[1]]
    share_out = share_two[:, w_fc.shape[1] :]
    small_share = share_one[:, 3 * model_width : 3 * model_width + small_count].T
    (
        share_gain_one,
        share_bias_one,
        share_bias_q,
        share_bias_v,
        share_bias_out,
        share_gain_two,
        share_bias_two,
        share_bias_proj,
    ) = [small_share[i] for i in range(8)]
    share_bias_fc = small_share[8:].reshape(-1)
    return (
        out_tokens,
        grad_inputs,
        share_gain_one,
        share_bias_one,
        share_qkv,
        share_bias_q,
        share_bias_v,
        share_out,
        share_bias_out,
        share_gain_two,
        share_bias_two,
        share_fc,
        share_bias_fc,
        share_proj,
        share_bias_proj,
    )


def solution(mesh):
    placed = (
        P("fsdp", "ctx", None, None),
        P("fsdp", None),
        P("fsdp"),
        P("fsdp"),
        P("fsdp", None),
        P("fsdp"),
        P("fsdp"),
        P("fsdp", None),
        P("fsdp"),
        P("fsdp"),
        P("fsdp"),
        P("fsdp", None),
        P("fsdp"),
        P("fsdp", None),
        P("fsdp"),
        P("fsdp", "ctx", None, None),
    )
    return jax.shard_map(
        body,
        mesh=mesh,
        in_specs=placed,
        out_specs=(
            P("fsdp", "ctx", None, None),
            P("fsdp", "ctx", None, None),
            P(("fsdp", "ctx")),
            P(("fsdp", "ctx")),
            P(("fsdp", "ctx"), None),
            P(("fsdp", "ctx")),
            P(("fsdp", "ctx")),
            P(("fsdp", "ctx"), None),
            P(("fsdp", "ctx")),
            P(("fsdp", "ctx")),
            P(("fsdp", "ctx")),
            P(("fsdp", "ctx"), None),
            P(("fsdp", "ctx")),
            P(("fsdp", "ctx"), None),
            P(("fsdp", "ctx")),
        ),
        check_vma=False,
    )
```

```python
import functools

import jax
import jax.numpy as jnp
from jax import lax
from jax.experimental import pallas as pl
from jax.experimental.pallas import tpu as pltpu
from jax.sharding import PartitionSpec as P

HEAD_DIM = 64
LANES = 128
EPSILON = 1e-05
NEG_FILL = -1e30
VMEM_BYTES = 56 * 1024 * 1024
LOW = jnp.bfloat16
FULL = jnp.float32
SMALL = 8
GELU_IN = 0.7978845608028654
GELU_CUBE = 0.044715


def dot_nt(left, right):
    return lax.dot_general(left, right, (((1,), (1,)), ((), ())), preferred_element_type=jnp.float32)


def dot_nn(left, right):
    return lax.dot_general(left, right, (((1,), (0,)), ((), ())), preferred_element_type=jnp.float32)


def dot_tn(left, right):
    return lax.dot_general(left, right, (((0,), (0,)), ((), ())), preferred_element_type=jnp.float32)


def swap_chip(value, count, mask):
    return lax.ppermute(value, "fsdp", [(i, i ^ mask) for i in range(count)])


def swap_core(value, count):
    return lax.ppermute(value, "ctx", [(i, i ^ 1) for i in range(count)])


def after(values, others):
    return lax.optimization_barrier((values, others))[0]


class Layout:
    def __init__(self, fsdp, n_ctx, rows):
        self.fsdp, self.n_ctx = fsdp, n_ctx
        self.merge = 0
        while (rows << self.merge) % 16:
            self.merge += 1
        self.rows = rows << self.merge
        self.chips = fsdp >> self.merge
        self.depth = self.chips // 4
        self.shares = n_ctx << self.merge

    def swap(self, value, offset):
        return swap_chip(value, self.fsdp, offset << self.merge)

    def merged(self, shard):
        for bit in range(self.merge):
            other = swap_chip(shard, self.fsdp, 1 << bit)
            first = ((lax.axis_index("fsdp") >> bit) & 1) == 0
            shard = jnp.concatenate([jnp.where(first, shard, other), jnp.where(first, other, shard)], axis=0)
        return shard


def gather_far(shard, lay, core):
    half = shard.shape[-1] // 2
    own = lax.dynamic_slice_in_dim(shard, core * half, half, 1)[None]
    return jnp.concatenate([own] + [lay.swap(own, 4 * j) for j in range(1, lay.depth)], axis=0)


def gather_near(held, lay):
    return held, lay.swap(held, 1), lay.swap(held, 2)


def gather_corner(near, lay):
    middle = lay.depth // 2
    return near + (lay.swap(near[2][:middle], 1), lay.swap(near[1][middle:], 2))


def gather_core(pieces, lay):
    return tuple(pieces) + tuple(swap_core(piece, lay.n_ctx) for piece in pieces)


def piece_offsets(lay):
    middle = lay.depth // 2
    whole = [[m ^ (4 * j) for j in range(lay.depth)] for m in range(4)]
    return [whole[0], whole[1], whole[2], whole[3][:middle], whole[3][middle:]]


def windows(lay, index_ref, half, blocks, model):
    chip, core = index_ref[0], index_ref[1]
    for other in (0, 1):
        side = (1 - core) if other else core
        for number, offsets in enumerate(piece_offsets(lay)):
            for place, offset in enumerate(offsets):
                origin = chip ^ offset
                if blocks == 1:
                    row = pl.multiple_of(origin * lay.rows, 16)
                    yield 5 * other + number, place, slice(None), pl.ds(row, lay.rows), pl.ds(pl.multiple_of(side * half, LANES), half)
                else:
                    for part in range(blocks // 2):
                        row = pl.multiple_of((origin * blocks + side * (blocks // 2) + part) * lay.rows, 16)
                        columns = slice(part * model, (part + 1) * model)
                        yield 5 * other + number, place, columns, pl.ds(row, lay.rows), slice(None)


def fill(whole, pieces, lay, index_ref, blocks=1):
    half = pieces[0].shape[2]
    for number, place, columns, row, column in windows(lay, index_ref, half, blocks, whole.shape[1]):
        whole[row, column] = pieces[number][place, :, columns]


def cut(whole, pieces, lay, index_ref, blocks=1):
    half = pieces[0].shape[2]
    for number, place, columns, row, column in windows(lay, index_ref, half, blocks, whole.shape[1]):
        pieces[number][place, :, columns] = whole[row, column]


def piece_shapes(lay, half):
    return [jax.ShapeDtypeStruct((len(offsets), lay.rows, half), LOW) for offsets in piece_offsets(lay)] * 2


def low_sum(*members):
    return sum(member.astype(FULL) for member in members).astype(LOW)


def scatter_core(pieces, lay):
    return tuple(low_sum(keep, swap_core(send, lay.n_ctx)) for keep, send in zip(pieces[:5], pieces[5:]))


def scatter_corner(sums, lay):
    middle = lay.depth // 2
    own, one, two, corner_low, corner_high = sums
    to_two = lay.swap(corner_low, 1)
    to_one = lay.swap(corner_high, 2)
    one = jnp.concatenate([one[:middle], low_sum(one[middle:], to_one)], axis=0)
    two = jnp.concatenate([low_sum(two[:middle], to_two), two[middle:]], axis=0)
    return own, one, two


def scatter_near(sums, lay):
    own, one, two = sums
    got_one, got_two = lay.swap(one, 1), lay.swap(two, 2)
    return [low_sum(own[j], got_one[j], got_two[j]) for j in range(lay.depth)]


def scatter_far(parts, lay):
    total = sum([parts[0].astype(FULL)] + [lay.swap(parts[j], 4 * j).astype(FULL) for j in range(1, lay.depth)])
    if lay.n_ctx > 2:
        groups = [list(range(0, lay.n_ctx, 2)), list(range(1, lay.n_ctx, 2))]
        total = lax.psum(total, "ctx", axis_index_groups=groups)
    for bit in range(lay.merge):
        total = total + swap_chip(total, lay.fsdp, 1 << bit)
    return total


def share_rows(total, lay, share):
    rows = total.shape[0] // lay.shares
    mine = lax.dynamic_slice_in_dim(total, share * rows, rows, 0)
    theirs = swap_core(lax.dynamic_slice_in_dim(total, (share ^ 1) * rows, rows, 0), lay.n_ctx)
    first = (share & 1) == 0
    return jnp.concatenate([jnp.where(first, mine, theirs), jnp.where(first, theirs, mine)], axis=1)


def share_blocks(total, lay, share, blocks):
    rows = total.shape[0]
    parts = blocks // 2
    if lay.shares > 2:
        parts = blocks
        theirs = swap_core(total, lay.n_ctx)
        first = (share & 1) == 0
        total = jnp.concatenate([jnp.where(first, total, theirs), jnp.where(first, theirs, total)], axis=1)
    stacked = jnp.moveaxis(total.reshape(rows, parts, -1), 1, 0).reshape(parts * rows, -1)
    if lay.shares > 2:
        count = stacked.shape[0] // lay.shares
        stacked = lax.dynamic_slice_in_dim(stacked, share * count, count, 0)
    return stacked


def call(kernel, out_shape, scalars, arrays, scratch=(), flops=0):
    moved = sum(member.size * member.dtype.itemsize for member in list(arrays) + list(out_shape))
    return pl.pallas_call(
        kernel,
        out_shape=out_shape,
        in_specs=[pl.BlockSpec(memory_space=pltpu.SMEM)] + [pl.BlockSpec(memory_space=pltpu.VMEM)] * len(arrays),
        out_specs=[pl.BlockSpec(memory_space=pltpu.VMEM)] * len(out_shape),
        scratch_shapes=list(scratch),
        compiler_params=pltpu.CompilerParams(vmem_limit_bytes=VMEM_BYTES),
        cost_estimate=pl.CostEstimate(flops=flops, bytes_accessed=moved, transcendentals=0),
    )(scalars, *arrays)


def shaped(rows, columns, dtype=LOW):
    return jax.ShapeDtypeStruct((rows, columns), dtype)


def normalised(values):
    average = jnp.mean(values, axis=-1, keepdims=True)
    centred = values - average
    scale = lax.rsqrt(jnp.mean(centred * centred, axis=-1, keepdims=True) + EPSILON)
    return centred * scale, scale


def normalised_back(grads, hat, scale):
    return (grads - jnp.mean(grads, axis=-1, keepdims=True) - hat * jnp.mean(grads * hat, axis=-1, keepdims=True)) * scale


def column_sum(values):
    return jnp.sum(values.astype(FULL), axis=0, keepdims=True)


def first_kernel(lay, index_ref, tokens, *refs):
    pieces, (normed_ref, query_ref, key_ref, value_ref, whole, small_ref) = refs[:10], refs[10:]
    model = tokens.shape[1]
    fill(whole, pieces, lay, index_ref)
    small = whole[:, 3 * model : 3 * model + LANES].astype(FULL).T
    small_ref[...] = small[: small_ref.shape[0], :]
    hat, scale = normalised(tokens[...].astype(FULL))
    normed = (hat * small_ref[0:1, :] + small_ref[1:2, :]).astype(LOW)
    normed_ref[...] = normed
    query_ref[...] = (dot_nn(normed, whole[:, :model]) + small_ref[2:3, :]).astype(LOW)
    key_ref[...] = dot_nn(normed, whole[:, model : 2 * model]).astype(LOW)
    value_ref[...] = (dot_nn(normed, whole[:, 2 * model : 3 * model]) + small_ref[3:4, :]).astype(LOW)


def hidden_kernel(lay, index_ref, mixed, tokens, small, fc_bias, *refs):
    pieces, (whole, middle_ref, normed_ref, active_ref, slope_ref) = refs[:10], refs[10:]
    model = tokens.shape[1]
    hidden = active_ref.shape[1]
    fill(whole, pieces, lay, index_ref)
    middle = tokens[...].astype(FULL) + dot_nn(mixed[...], whole[:, hidden:]) + small[4:5, :]
    middle_ref[...] = middle
    hat, scale = normalised(middle)
    normed = (hat * small[5:6, :] + small[6:7, :]).astype(LOW)
    normed_ref[...] = normed
    for start in range(0, hidden, model):
        columns = slice(start, start + model)
        pre = dot_nn(normed, whole[:, columns]) + fc_bias[:, columns]
        square = pre * pre
        bent = jnp.tanh(GELU_IN * (pre + GELU_CUBE * square * pre))
        active_ref[:, columns] = (0.5 * pre * (1.0 + bent)).astype(LOW)
        slope = 0.5 * (1.0 + bent) + 0.5 * pre * (1.0 - bent * bent) * (GELU_IN * (1.0 + 3.0 * GELU_CUBE * square))
        slope_ref[:, columns] = slope.astype(LOW)


def proj_grad_kernel(lay, blocks, index_ref, active, cotangent, *refs):
    pieces, (sum_ref, whole) = refs[:10], refs[10:]
    model = cotangent.shape[1]
    sum_ref[...] = column_sum(cotangent[...])
    for start in range(0, active.shape[1], model):
        columns = slice(start, start + model)
        whole[columns, :] = dot_tn(active[:, columns], cotangent[...]).astype(LOW)
    cut(whole, pieces, lay, index_ref, blocks)


def middle_kernel(lay, blocks, index_ref, active, slope, cotangent, middle_ref, small, weights, *refs):
    pieces = refs[:10]
    out_ref, d_pre_ref, d_middle_ref, d_branch_ref, d_mixed_ref, sums_ref, hidden_sums_ref, proj = refs[10:]
    model = cotangent.shape[1]
    hidden = active.shape[1]
    fill(proj, pieces, lay, index_ref, blocks)
    d_normed = None
    for start in range(0, hidden, model):
        columns = slice(start, start + model)
        d_active = dot_nt(cotangent[...], proj[columns, :])
        d_pre = (d_active * slope[:, columns].astype(FULL)).astype(LOW)
        d_pre_ref[:, columns] = d_pre
        hidden_sums_ref[:, columns] = column_sum(d_pre)
        part = dot_nt(d_pre, weights[:, columns])
        d_normed = part if d_normed is None else d_normed + part
    hat, scale = normalised(middle_ref[...])
    sums_ref[0:1, :] = column_sum(d_normed * hat)
    sums_ref[1:2, :] = column_sum(d_normed)
    d_middle = cotangent[...].astype(FULL) + normalised_back(d_normed * small[5:6, :], hat, scale)
    d_middle_ref[...] = d_middle
    d_branch = d_middle.astype(LOW)
    d_branch_ref[...] = d_branch
    sums_ref[2:3, :] = column_sum(d_branch)
    d_mixed_ref[...] = dot_nt(d_branch, weights[:, hidden:]).astype(LOW)
    out_ref[...] = (middle_ref[...] + dot_nn(active[...], proj[...]) + small[7:8, :]).astype(LOW)


def hidden_grad_kernel(lay, index_ref, normed, d_pre, mixed, d_branch, *refs):
    pieces, whole = refs[:10], refs[10]
    model = normed.shape[1]
    hidden = d_pre.shape[1]
    for start in range(0, hidden, model):
        columns = slice(start, start + model)
        whole[:, columns] = dot_tn(normed[...], d_pre[:, columns]).astype(LOW)
    whole[:, hidden:] = dot_tn(mixed[...], d_branch[...]).astype(LOW)
    cut(whole, pieces, lay, index_ref)


def last_kernel(lay, count, index_ref, tokens, small, normed, weights, d_middle, others, *refs):
    backs = refs[: 5 * count]
    pieces = refs[5 * count : 5 * count + 10]
    grad_ref, d_qkv, whole, sums = refs[5 * count + 10 :]
    model = tokens.shape[1]
    at = 0
    for number in range(count):
        d_query, d_key, d_key_got, d_value, d_value_got = backs[5 * number : 5 * number + 5]
        width = d_query.shape[1]
        d_qkv[:, at : at + width] = d_query[...]
        d_qkv[:, model + at : model + at + width] = (d_key[...].astype(FULL) + d_key_got[...].astype(FULL)).astype(LOW)
        d_qkv[:, 2 * model + at : 2 * model + at + width] = (
            d_value[...].astype(FULL) + d_value_got[...].astype(FULL)
        ).astype(LOW)
        at += width
    d_normed = dot_nt(d_qkv[...], weights[:, : 3 * model])
    hat, scale = normalised(tokens[...].astype(FULL))
    grad_ref[...] = d_middle[...] + normalised_back(d_normed * small[0:1, :], hat, scale)
    sums[...] = jnp.zeros_like(sums)
    sums[0 : others.shape[0], :] = others[...]
    sums[0:1, :] = column_sum(d_normed * hat)
    sums[1:2, :] = column_sum(d_normed)
    sums[2:3, :] = column_sum(d_qkv[:, :model])
    sums[3:4, :] = column_sum(d_qkv[:, 2 * model :])
    for start in range(0, 3 * model, model):
        columns = slice(start, start + model)
        whole[:, columns] = dot_tn(normed[...], d_qkv[:, columns]).astype(LOW)
    whole[:, 3 * model : 3 * model + LANES] = sums[...].T.astype(LOW)
    whole[:, 3 * model + LANES :] = jnp.zeros((model, whole.shape[1] - 3 * model - LANES), LOW)
    cut(whole, pieces, lay, index_ref)


def head_lanes(head):
    lanes = lax.broadcasted_iota(jnp.int32, (1, 2 * HEAD_DIM), 1)
    return (lanes < HEAD_DIM) if head == 0 else (lanes >= HEAD_DIM)


def at_or_before(block):
    query_at = lax.broadcasted_iota(jnp.int32, (block, block), 0)
    key_at = lax.broadcasted_iota(jnp.int32, (block, block), 1)
    return query_at >= key_at


def softmax_parts(scores, values):
    top = functools.reduce(jnp.maximum, [jnp.max(s, axis=1, keepdims=True) for s in scores])
    weights = [jnp.exp(s - top) for s in scores]
    total = sum(jnp.sum(w, axis=1, keepdims=True) for w in weights)
    out = sum(dot_nn(w.astype(jnp.bfloat16), v) for w, v in zip(weights, values))
    return top, total, out


def merge_parts(left, right):
    top = jnp.maximum(left[0], right[0])
    left_scale, right_scale = jnp.exp(left[0] - top), jnp.exp(right[0] - top)
    return (
        top,
        left[1] * left_scale + right[1] * right_scale,
        left[2] * left_scale + right[2] * right_scale,
    )


def attend_kernel(n_ctx, early_ref, query_ref, own_key, own_value, far_key, far_value, out_ref, lse_ref):
    block = query_ref.shape[0] // 2
    causal = at_or_before(block)
    results = []
    for head in (0, 1):
        lanes = head_lanes(head)
        zero = jnp.zeros((), jnp.bfloat16)

        def rows_of(start):
            return jnp.where(lanes, query_ref[pl.ds(start, block), :] * HEAD_DIM**-0.5, zero)

        def keys_of(start, far=False):
            return (far_key if far else own_key)[pl.ds(start, block), :]

        def values_of(start, far=False):
            return (far_value if far else own_value)[pl.ds(start, block), :]

        query_low, query_high = rows_of(0), rows_of(block)
        low = softmax_parts([jnp.where(causal, dot_nt(query_low, keys_of(0)), NEG_FILL)], [values_of(0)])
        seen = [(0, False)] + [(2 * other * block, True) for other in range(n_ctx - 1)]
        high = softmax_parts(
            [jnp.where(causal, dot_nt(query_high, keys_of(block)), NEG_FILL)]
            + [dot_nt(query_high, keys_of(*at)) for at in seen],
            [values_of(block)] + [values_of(*at) for at in seen],
        )
        for other in range(n_ctx - 1):
            early = early_ref[other + 1]
            query_at = pl.multiple_of((1 - early) * block, block)
            key_at = pl.multiple_of((2 * other + 1 - early) * block, block)
            top, total, out = softmax_parts([dot_nt(rows_of(query_at), keys_of(key_at, True))], [values_of(key_at, True)])
            low = merge_parts(low, (jnp.where(early == 1, top, NEG_FILL), total, out))
            high = merge_parts(high, (jnp.where(early == 1, NEG_FILL, top), total, out))
        results.append((low, high))
    lanes = head_lanes(0)
    for half in (0, 1):
        (top_a, total_a, out_a), (top_b, total_b, out_b) = results[0][half], results[1][half]
        rows = pl.ds(half * block, block)
        out_ref[rows, :] = jnp.where(lanes, out_a / total_a, out_b / total_b).astype(out_ref.dtype)
        lse_ref[rows, :] = jnp.where(lanes, top_a + jnp.log(total_a), top_b + jnp.log(total_b))


def attend_back_kernel(
    n_ctx,
    early_ref,
    query_ref,
    own_key,
    own_value,
    far_key,
    far_value,
    dmix_ref,
    out_ref,
    lse_ref,
    dq_ref,
    dk_ref,
    dv_ref,
    far_dk_ref,
    far_dv_ref,
    dq_sum,
    dk_own,
    dv_own,
    dk_far,
    dv_far,
):
    block = query_ref.shape[0] // 2
    causal = at_or_before(block)
    zero = jnp.zeros((), jnp.bfloat16)
    for total in (dq_sum, dk_own, dv_own, dk_far, dv_far):
        total[...] = jnp.zeros_like(total)
    for head in (0, 1):
        lanes = head_lanes(head)

        def pair(query_at, key_at, mask=None, far=False):
            key_ref, value_ref, dk_sum, dv_sum = (
                (far_key, far_value, dk_far, dv_far) if far else (own_key, own_value, dk_own, dv_own)
            )
            query_rows, key_rows = pl.ds(query_at, block), pl.ds(key_at, block)
            query = jnp.where(lanes, query_ref[query_rows, :] * HEAD_DIM**-0.5, zero)
            dmix = jnp.where(lanes, dmix_ref[query_rows, :], zero)
            keys = key_ref[key_rows, :]
            product = dmix.astype(jnp.float32) * out_ref[query_rows, :].astype(jnp.float32)
            delta = jnp.sum(product, axis=1, keepdims=True)
            lse = lse_ref[query_rows, head * HEAD_DIM : head * HEAD_DIM + 1]
            chances = jnp.exp(dot_nt(query, keys) - lse)
            if mask is not None:
                chances = jnp.where(mask, chances, 0.0)
            d_scores = (chances * (dot_nt(dmix, value_ref[key_rows, :]) - delta)).astype(jnp.bfloat16)
            dq_sum[query_rows, :] += dot_nn(d_scores, jnp.where(lanes, keys, zero))
            dk_sum[key_rows, :] += dot_tn(d_scores, query)
            dv_sum[key_rows, :] += dot_tn(chances.astype(jnp.bfloat16), dmix)

        pair(0, 0, causal)
        pair(block, block, causal)
        pair(block, 0)
        for other in range(n_ctx - 1):
            pair(block, 2 * other * block, far=True)
            early = early_ref[other + 1]
            pair(
                pl.multiple_of((1 - early) * block, block),
                pl.multiple_of((2 * other + 1 - early) * block, block),
                far=True,
            )
    dq_ref[...] = (dq_sum[...] * HEAD_DIM**-0.5).astype(dq_ref.dtype)
    for target, total in ((dk_ref, dk_own), (dv_ref, dv_own), (far_dk_ref, dk_far), (far_dv_ref, dv_far)):
        target[...] = total[...].astype(target.dtype)


def pair_spec(rows, start=0):
    return pl.BlockSpec((rows, 2 * HEAD_DIM), lambda pair: (0, start + pair))


def pair_spec(rows, start=0):
    return pl.BlockSpec((rows, 2 * HEAD_DIM), lambda pair: (0, start + pair))


def attend(early, queries, context, n_ctx):
    length, width = queries.shape
    return pl.pallas_call(
        functools.partial(attend_kernel, n_ctx),
        grid=(width // (2 * HEAD_DIM),),
        out_shape=[shaped(length, width), shaped(length, width, FULL)],
        in_specs=[pl.BlockSpec(memory_space=pltpu.SMEM)] + [pair_spec(member.shape[0]) for member in (queries,) + context],
        out_specs=[pair_spec(length)] * 2,
        compiler_params=pltpu.CompilerParams(vmem_limit_bytes=VMEM_BYTES),
        cost_estimate=pl.CostEstimate(
            flops=8 * n_ctx * length * length * width, bytes_accessed=14 * length * width, transcendentals=length * length * n_ctx
        ),
    )(early, queries, *context)


def attend_back(early, queries, context, dmix, out, lse, n_ctx, start, stop):
    length = queries.shape[0]
    others = context[2].shape[0]
    span = (stop - start) * 2 * HEAD_DIM
    operands = (queries,) + context + (dmix, out, lse)
    heights = [length, length, length, others, others]
    return pl.pallas_call(
        functools.partial(attend_back_kernel, n_ctx),
        grid=(stop - start,),
        out_shape=[shaped(height, span) for height in heights],
        in_specs=[pl.BlockSpec(memory_space=pltpu.SMEM)] + [pair_spec(member.shape[0], start) for member in operands],
        out_specs=[pair_spec(height) for height in heights],
        scratch_shapes=[pltpu.VMEM((height, 2 * HEAD_DIM), FULL) for height in heights],
        compiler_params=pltpu.CompilerParams(vmem_limit_bytes=VMEM_BYTES),
        cost_estimate=pl.CostEstimate(
            flops=20 * n_ctx * length * length * span, bytes_accessed=20 * length * span, transcendentals=length * length * n_ctx
        ),
    )(early, *operands)


def gather_ctx(own, n_ctx, ctx_index):
    if n_ctx == 2:
        return swap_core(own, n_ctx)
    whole = lax.all_gather(own, "ctx", axis=0, tiled=True)
    return jnp.roll(whole, -ctx_index * own.shape[0], axis=0)[own.shape[0] :]


def scatter_ctx(own, far, n_ctx, ctx_index):
    if n_ctx == 2:
        return own, swap_core(far, n_ctx)
    whole = jnp.roll(jnp.concatenate([own, far], axis=0), ctx_index * own.shape[0], axis=0)
    return lax.psum_scatter(whole, "ctx", scatter_dimension=0, tiled=True), jnp.zeros_like(own)


def body(
    tokens,
    pair_order,
    gain_one,
    bias_one,
    w_qkv,
    bias_q,
    bias_v,
    w_out,
    bias_out,
    gain_two,
    bias_two,
    w_fc,
    bias_fc,
    w_proj,
    bias_proj,
    cotangent,
):
    model = tokens.shape[-1]
    length = tokens.shape[2]
    fsdp, n_ctx = lax.axis_size("fsdp"), lax.axis_size("ctx")
    ctx_index = lax.axis_index("ctx")
    core = ctx_index & 1
    chip = lax.axis_index("fsdp")
    lay = Layout(fsdp, n_ctx, gain_one.shape[0])
    share = (chip & ((1 << lay.merge) - 1)) * n_ctx + ctx_index
    where = jnp.stack([chip >> lay.merge, core]).astype(jnp.int32)
    rows, depth = lay.rows, lay.depth
    tokens_in = tokens.reshape(length, model)
    cotangent_in = cotangent.reshape(length, model)
    vectors = [gain_one, bias_one, bias_q, bias_v, bias_out, gain_two, bias_two, bias_proj]
    bias_rows = lay.merged(bias_fc).reshape(-1, rows)
    blocks = bias_rows.shape[0]
    small_count = SMALL + blocks
    small_rows = jnp.concatenate([lay.merged(jnp.stack(vectors, axis=1)), bias_rows.T], axis=1)
    small_rows = jnp.pad(small_rows, ((0, 0), (0, 2 * LANES - small_count)))
    hidden = w_fc.shape[1]
    group_one = jnp.concatenate([lay.merged(w_qkv), small_rows], axis=1)
    group_two = jnp.concatenate([lay.merged(w_fc), lay.merged(w_out)], axis=1)
    group_three = jnp.moveaxis(lay.merged(w_proj).reshape(blocks, rows, model), 0, 1).reshape(rows, blocks * model)
    half_one, half_two, half_three = [member.shape[1] // 2 for member in (group_one, group_two, group_three)]

    far_one = gather_far(group_one, lay, core)
    group_two, group_three = after((group_two, group_three), far_one)
    far_two = gather_far(group_two, lay, core)
    near_one = gather_near(far_one, lay)
    corner_one = gather_corner(near_one, lay)
    corner_one, far_two, group_three = lax.optimization_barrier((corner_one, far_two, group_three))
    near_two = gather_near(far_two, lay)
    far_three = gather_far(group_three, lay, core)
    normed_one, queries, keys, values, whole_one, small = call(
        functools.partial(first_kernel, lay),
        [shaped(length, model)] * 4 + [shaped(model, 2 * half_one), shaped(16, model, FULL)],
        where,
        (tokens_in,) + gather_core(corner_one, lay),
        flops=6 * length * model * model,
    )
    context = (keys, values, gather_ctx(keys, n_ctx, ctx_index), gather_ctx(values, n_ctx, ctx_index))
    context, near_two, far_three = lax.optimization_barrier((context, near_two, far_three))
    corner_two = gather_corner(near_two, lay)
    pairs = jnp.roll(pair_order[0], -ctx_index)
    early = (pairs < pairs[0]).astype(jnp.int32)
    mixed, lse = attend(early, queries, context, n_ctx)
    mixed, corner_two, far_three = lax.optimization_barrier((mixed, corner_two, far_three))
    near_three = gather_near(far_three, lay)
    fc_bias = jnp.moveaxis(small[SMALL:small_count].reshape(blocks, lay.chips, rows), 0, 1).reshape(1, hidden)
    whole_two, middle, normed_two, active, slope = call(
        functools.partial(hidden_kernel, lay),
        [
            shaped(model, 2 * half_two),
            shaped(length, model, FULL),
            shaped(length, model),
            shaped(length, hidden),
            shaped(length, hidden),
        ],
        where,
        (mixed, tokens_in, small, fc_bias) + gather_core(corner_two, lay),
        flops=2 * length * model * (model + hidden),
    )
    active, near_three = lax.optimization_barrier((active, near_three))
    corner_three = gather_corner(near_three, lay)
    *share_three, sum_cotangent = call(
        functools.partial(proj_grad_kernel, lay, blocks),
        piece_shapes(lay, half_three) + [shaped(1, model, FULL)],
        where,
        (active, cotangent_in),
        [pltpu.VMEM((hidden, model), LOW)],
        flops=2 * length * model * hidden,
    )
    share_three, corner_three = lax.optimization_barrier((share_three, corner_three))
    share_three = scatter_core(share_three, lay)
    out_rows, d_pre, d_middle, d_branch, d_mixed, sums, hidden_sums = call(
        functools.partial(middle_kernel, lay, blocks),
        [
            shaped(length, model),
            shaped(length, hidden),
            shaped(length, model, FULL),
            shaped(length, model),
            shaped(length, model),
            shaped(8, model, FULL),
            shaped(1, hidden, FULL),
        ],
        where,
        (active, slope, cotangent_in, middle, small, whole_two) + gather_core(corner_three, lay),
        [pltpu.VMEM((hidden, model), LOW)],
        flops=6 * length * model * hidden,
    )
    share_three = scatter_corner(share_three, lay)
    d_pre, share_three = lax.optimization_barrier((d_pre, share_three))
    share_three = scatter_near(share_three, lay)
    share_two = call(
        functools.partial(hidden_grad_kernel, lay),
        piece_shapes(lay, half_two),
        where,
        (normed_two, d_pre, mixed, d_branch),
        [pltpu.VMEM((model, 2 * half_two), LOW)],
        flops=2 * length * model * (model + hidden),
    )
    d_mixed, share_two, share_three = lax.optimization_barrier((d_mixed, share_two, share_three))
    share_two = scatter_core(share_two, lay)
    total_three = scatter_far(share_three, lay)
    share_two = scatter_corner(share_two, lay)
    pair_count = model // (2 * HEAD_DIM)
    cuts = [0, pair_count // 3, pair_count]
    backs = []
    for start, stop in zip(cuts[:-1], cuts[1:]):
        d_query, d_key, d_value, far_key, far_value = attend_back(
            early, queries, context, d_mixed, mixed, lse, n_ctx, start, stop
        )
        backs.append(
            (d_query,) + scatter_ctx(d_key, far_key, n_ctx, ctx_index) + scatter_ctx(d_value, far_value, n_ctx, ctx_index)
        )
        if start == 0:
            d_mixed, share_two, total_three, d_query = lax.optimization_barrier((d_mixed, share_two, total_three, d_query))
            share_two = scatter_near(share_two, lay)
    backs, share_two = lax.optimization_barrier((backs, share_two))
    total_two = scatter_far(share_two, lay)
    others = jnp.concatenate(
        [
            jnp.zeros((4, model), FULL),
            sums[2:3],
            sums[0:2],
            sum_cotangent,
            jnp.moveaxis(hidden_sums.reshape(lay.chips, lay.shares, blocks, rows // lay.shares), 2, 0).reshape(blocks, model),
            jnp.zeros((16 - small_count, model), FULL),
        ]
    )
    *share_one, grad_rows = call(
        functools.partial(last_kernel, lay, len(backs)),
        piece_shapes(lay, half_one) + [shaped(length, model, FULL)],
        where,
        (tokens_in, small, normed_one, whole_one, d_middle, others) + sum(backs, ()),
        [
            pltpu.VMEM((length, 3 * model), LOW),
            pltpu.VMEM((model, 2 * half_one), LOW),
            pltpu.VMEM((LANES, model), FULL),
        ],
        flops=12 * length * model * model,
    )
    share_one = scatter_core(share_one, lay)
    share_one = scatter_corner(share_one, lay)
    share_one = scatter_near(share_one, lay)
    share_one = share_rows(scatter_far(share_one, lay), lay, share)
    share_two = share_rows(total_two, lay, share)
    share_proj = share_blocks(total_three, lay, share, blocks)
    small_share = share_one[:, 3 * model : 3 * model + small_count].T
    names = ("gain_one", "bias_one", "bias_q", "bias_v", "bias_out", "gain_two", "bias_two", "bias_proj")
    small_grads = dict(zip(names, small_share))
    return (
        out_rows.reshape(tokens.shape),
        grad_rows.reshape(tokens.shape),
        small_grads["gain_one"],
        small_grads["bias_one"],
        share_one[:, : 3 * model],
        small_grads["bias_q"],
        small_grads["bias_v"],
        share_two[:, hidden:],
        small_grads["bias_out"],
        small_grads["gain_two"],
        small_grads["bias_two"],
        share_two[:, :hidden],
        small_share[SMALL:].reshape(-1),
        share_proj,
        small_grads["bias_proj"],
    )


def solution(mesh):
    placed = (
        P("fsdp", "ctx", None, None),
        P("fsdp", None),
        P("fsdp"),
        P("fsdp"),
        P("fsdp", None),
        P("fsdp"),
        P("fsdp"),
        P("fsdp", None),
        P("fsdp"),
        P("fsdp"),
        P("fsdp"),
        P("fsdp", None),
        P("fsdp"),
        P("fsdp", None),
        P("fsdp"),
        P("fsdp", "ctx", None, None),
    )
    return jax.shard_map(
        body,
        mesh=mesh,
        in_specs=placed,
        out_specs=(
            P("fsdp", "ctx", None, None),
            P("fsdp", "ctx", None, None),
            P(("fsdp", "ctx")),
            P(("fsdp", "ctx")),
            P(("fsdp", "ctx"), None),
            P(("fsdp", "ctx")),
            P(("fsdp", "ctx")),
            P(("fsdp", "ctx"), None),
            P(("fsdp", "ctx")),
            P(("fsdp", "ctx")),
            P(("fsdp", "ctx")),
            P(("fsdp", "ctx"), None),
            P(("fsdp", "ctx")),
            P(("fsdp", "ctx"), None),
            P(("fsdp", "ctx")),
        ),
        check_vma=False,
    )
```

```python
import functools

import jax
import jax.numpy as jnp
from jax import lax
from jax.experimental import pallas as pl
from jax.experimental.pallas import tpu as pltpu
from jax.sharding import PartitionSpec as P

HEAD_DIM = 64
LANES = 128
EPSILON = 1e-05
NEG_FILL = -1e30
VMEM_BYTES = 56 * 1024 * 1024
LOW = jnp.bfloat16
FULL = jnp.float32
SMALL = 8
GELU_IN = 0.7978845608028654
GELU_CUBE = 0.044715


def dot_nt(left, right):
    return lax.dot_general(left, right, (((1,), (1,)), ((), ())), preferred_element_type=jnp.float32)


def dot_nn(left, right):
    return lax.dot_general(left, right, (((1,), (0,)), ((), ())), preferred_element_type=jnp.float32)


def dot_tn(left, right):
    return lax.dot_general(left, right, (((0,), (0,)), ((), ())), preferred_element_type=jnp.float32)


def swap_chip(value, count, mask):
    return lax.ppermute(value, "fsdp", [(i, i ^ mask) for i in range(count)])


def swap_core(value, count):
    return lax.ppermute(value, "ctx", [(i, i ^ 1) for i in range(count)])


def after(values, others):
    return lax.optimization_barrier((values, others))[0]


class Layout:
    def __init__(self, fsdp, n_ctx, rows):
        self.fsdp, self.n_ctx = fsdp, n_ctx
        self.merge = 0
        while (rows << self.merge) % 16:
            self.merge += 1
        self.rows = rows << self.merge
        self.chips = fsdp >> self.merge
        self.depth = self.chips // 4
        self.shares = n_ctx << self.merge

    def swap(self, value, offset):
        return swap_chip(value, self.fsdp, offset << self.merge)

    def merged(self, shard):
        for bit in range(self.merge):
            other = swap_chip(shard, self.fsdp, 1 << bit)
            first = ((lax.axis_index("fsdp") >> bit) & 1) == 0
            shard = jnp.concatenate([jnp.where(first, shard, other), jnp.where(first, other, shard)], axis=0)
        return shard


def half_of(shards, core):
    halves = [
        lax.dynamic_slice_in_dim(shard, core * (shard.shape[1] // 2), shard.shape[1] // 2, 1) for shard in shards
    ]
    return jnp.concatenate(halves, axis=1)[None]


def far_steps(lay):
    return range(1, lay.depth - 1), range(lay.depth - 1, lay.depth)


def gather_far(own, lay, steps):
    return [lay.swap(own, 4 * j) for j in steps]


def gather_near(far, lay):
    held = jnp.concatenate(far, axis=0)
    return held, lay.swap(held, 1), lay.swap(held, 2)


def gather_corner(near, lay):
    middle = lay.depth // 2
    return lay.swap(near[2][:middle], 1), lay.swap(near[1][middle:], 2)


def core_of(pieces, lay):
    return tuple(swap_core(piece, lay.n_ctx) for piece in pieces)


def piece_offsets(lay):
    middle = lay.depth // 2
    whole = [[m ^ (4 * j) for j in range(lay.depth)] for m in range(4)]
    return [whole[0], whole[1], whole[2], whole[3][:middle], whole[3][middle:]]


def windows(lay, index_ref, rows, widths, sides):
    chip, core = index_ref[0], index_ref[1]
    for other in range(sides):
        side = (1 - core) if other else core
        for number, offsets in enumerate(piece_offsets(lay)):
            for place, offset in enumerate(offsets):
                row = pl.ds(pl.multiple_of((chip ^ offset) * rows, 16), rows)
                at = 0
                for width in widths:
                    column = pl.ds(pl.multiple_of(2 * at + side * width, LANES), width)
                    yield 5 * other + number, place, slice(at, at + width), row, column
                    at += width


def fill(whole, pieces, lay, index_ref, widths):
    for number, place, columns, row, column in windows(lay, index_ref, pieces[0].shape[1], widths, 2):
        whole[row, column] = pieces[number][place, :, columns]


def cut(whole, pieces, lay, index_ref):
    rows = pieces[0].shape[1]
    chip = index_ref[0]
    for number, offsets in enumerate(piece_offsets(lay)):
        for place, offset in enumerate(offsets):
            pieces[number][place] = whole[pl.ds(pl.multiple_of((chip ^ offset) * rows, 16), rows), :]


def piece_shapes(lay, rows, half):
    return [jax.ShapeDtypeStruct((len(offsets), rows, half), LOW) for offsets in piece_offsets(lay)]


def low_sum(*members):
    return sum(member.astype(FULL) for member in members).astype(LOW)


def scatter_corner(sums, lay):
    return tuple(sums[:3]) + (lay.swap(sums[3], 1), lay.swap(sums[4], 2))


def scatter_near_sums(sums, lay):
    middle = lay.depth // 2
    own, one, two, to_two, to_one = sums
    return own, (one[:middle], low_sum(two[:middle], to_two)), (low_sum(one[middle:], to_one), two[middle:])


def scatter_near(pair, lay):
    return lay.swap(pair[0], 1), lay.swap(pair[1], 2)


def scatter_far_parts(own, low, high, lay):
    middle = lay.depth // 2
    return [
        low_sum(own[j], *(member[j if j < middle else j - middle] for member in (low if j < middle else high)))
        for j in range(lay.depth)
    ]


def scatter_far(parts, lay, steps):
    return [lay.swap(parts[j], 4 * j) for j in steps]


def scatter_end(parts, lay):
    total = sum(part.astype(FULL) for part in parts)
    if lay.n_ctx > 2:
        groups = [list(range(0, lay.n_ctx, 2)), list(range(1, lay.n_ctx, 2))]
        total = lax.psum(total, "ctx", axis_index_groups=groups)
    for bit in range(lay.merge):
        total = total + swap_chip(total, lay.fsdp, 1 << bit)
    return total


def share_rows(total, lay, share):
    rows = total.shape[0] // lay.shares
    mine = lax.dynamic_slice_in_dim(total, share * rows, rows, 0)
    theirs = swap_core(lax.dynamic_slice_in_dim(total, (share ^ 1) * rows, rows, 0), lay.n_ctx)
    first = (share & 1) == 0
    return jnp.where(first, mine, theirs), jnp.where(first, theirs, mine)


def call(kernel, out_shape, scalars, arrays, scratch=(), flops=0):
    moved = sum(member.size * member.dtype.itemsize for member in list(arrays) + list(out_shape))
    return pl.pallas_call(
        kernel,
        out_shape=out_shape,
        in_specs=[pl.BlockSpec(memory_space=pltpu.SMEM)] + [pl.BlockSpec(memory_space=pltpu.VMEM)] * len(arrays),
        out_specs=[pl.BlockSpec(memory_space=pltpu.VMEM)] * len(out_shape),
        scratch_shapes=list(scratch),
        compiler_params=pltpu.CompilerParams(vmem_limit_bytes=VMEM_BYTES),
        cost_estimate=pl.CostEstimate(flops=3 * flops, bytes_accessed=moved, transcendentals=0),
    )(scalars, *arrays)


def shaped(rows, columns, dtype=LOW):
    return jax.ShapeDtypeStruct((rows, columns), dtype)


def normalised(values):
    average = jnp.mean(values, axis=-1, keepdims=True)
    centred = values - average
    scale = lax.rsqrt(jnp.mean(centred * centred, axis=-1, keepdims=True) + EPSILON)
    return centred * scale, scale


def normalised_back(grads, hat, scale):
    return (grads - jnp.mean(grads, axis=-1, keepdims=True) - hat * jnp.mean(grads * hat, axis=-1, keepdims=True)) * scale


def column_sum(values):
    return jnp.sum(values.astype(FULL), axis=0, keepdims=True)


def half_at(ref, side):
    width = ref.shape[1] // 2
    return ref[:, pl.ds(pl.multiple_of(side * width, LANES), width)]


def first_kernel(lay, widths, index_ref, tokens, *refs):
    pieces, (normed_ref, query_ref, both_ref, whole, small_ref) = refs[:10], refs[10:]
    model = tokens.shape[1]
    fill(whole, pieces, lay, index_ref, widths)
    small = whole[:, 3 * model : 3 * model + LANES].astype(FULL).T
    small_ref[...] = small[: small_ref.shape[0], :]
    hat, scale = normalised(tokens[...].astype(FULL))
    normed = (hat * small_ref[0:1, :] + small_ref[1:2, :]).astype(LOW)
    normed_ref[...] = normed
    length = normed.shape[0]
    both_ref[:length, :] = dot_nn(normed, whole[:, model : 2 * model]).astype(LOW)
    both_ref[length:, :] = (dot_nn(normed, whole[:, 2 * model : 3 * model]) + small_ref[3:4, :]).astype(LOW)
    query_ref[...] = (dot_nn(normed, whole[:, :model]) + small_ref[2:3, :]).astype(LOW)


def hidden_kernel(lay, widths, index_ref, mixed, tokens, small, fc_bias, *refs):
    pieces, (middle_ref, normed_ref, active_ref, slope_ref, whole) = refs[:10], refs[10:]
    model = tokens.shape[1]
    hidden = active_ref.shape[1]
    fill(whole, pieces, lay, index_ref, widths)
    middle = tokens[...].astype(FULL) + dot_nn(mixed[...], whole[:, hidden:]) + small[4:5, :]
    middle_ref[...] = middle
    hat, scale = normalised(middle)
    normed = (hat * small[5:6, :] + small[6:7, :]).astype(LOW)
    normed_ref[...] = normed
    for start in range(0, hidden, model):
        columns = slice(start, start + model)
        pre = dot_nn(normed, whole[:, columns]) + fc_bias[:, columns]
        square = pre * pre
        part = 0.5 + 0.5 * jnp.tanh(pre * (GELU_IN + GELU_IN * GELU_CUBE * square))
        active = pre * part
        active_ref[:, columns] = active.astype(LOW)
        slope = part + active * (1.0 - part) * (2.0 * GELU_IN + 6.0 * GELU_IN * GELU_CUBE * square)
        slope_ref[:, columns] = slope.astype(LOW)


def proj_grad_kernel(lay, index_ref, active, active_far, cotangent, cotangent_far, *refs):
    pieces, (sum_ref, whole) = refs[:5], refs[5:]
    model = cotangent.shape[1]
    core = index_ref[1]
    sum_ref[...] = column_sum(cotangent[...])
    own, far = half_at(cotangent, core), half_at(cotangent_far, core)
    for start in range(0, active.shape[1], model):
        columns = slice(start, start + model)
        whole[columns, :] = (dot_tn(active[:, columns], own) + dot_tn(active_far[:, columns], far)).astype(LOW)
    cut(whole, pieces, lay, index_ref)


def middle_kernel(lay, widths, index_ref, cotangent, *refs):
    core = index_ref[1]
    proj_pieces, slope, pieces, (middle_ref, small, active), refs = refs[:10], refs[10], refs[11:21], refs[21:24], refs[24:]
    out_ref, keep_ref, send_ref, d_middle_ref, d_mixed_ref, sums_ref, hidden_sums_ref = refs[:7]
    proj, weights, d_pre_all, d_branch_all = refs[7:]
    model = cotangent.shape[1]
    hidden = active.shape[1]
    fill(proj, proj_pieces, lay, index_ref, (model // 2,))
    d_normed = None
    for start in range(0, hidden, model):
        columns = slice(start, start + model)
        d_active = dot_nt(cotangent[...], proj[columns, :])
        d_pre = (d_active * slope[:, columns].astype(FULL)).astype(LOW)
        d_pre_all[:, columns] = d_pre
        hidden_sums_ref[:, columns] = column_sum(d_pre)
        if start == 0:
            fill(weights, pieces, lay, index_ref, widths)
        part = dot_nt(d_pre, weights[:, columns])
        d_normed = part if d_normed is None else d_normed + part
    keep_ref[:, : hidden // 2] = half_at(d_pre_all, core)
    send_ref[:, : hidden // 2] = half_at(d_pre_all, 1 - core)
    hat, scale = normalised(middle_ref[...])
    sums_ref[0:1, :] = column_sum(d_normed * hat)
    sums_ref[1:2, :] = column_sum(d_normed)
    d_middle = cotangent[...].astype(FULL) + normalised_back(d_normed * small[5:6, :], hat, scale)
    d_middle_ref[...] = d_middle
    d_branch = d_middle.astype(LOW)
    d_branch_all[...] = d_branch
    keep_ref[:, hidden // 2 :] = half_at(d_branch_all, core)
    send_ref[:, hidden // 2 :] = half_at(d_branch_all, 1 - core)
    sums_ref[2:3, :] = column_sum(d_branch)
    d_mixed_ref[...] = dot_nt(d_branch, weights[:, hidden:]).astype(LOW)
    out_ref[...] = (middle_ref[...] + dot_nn(active[...], proj[...]) + small[7:8, :]).astype(LOW)


def hidden_grad_kernel(lay, widths, index_ref, normed, normed_far, mixed, mixed_far, keep, got, *refs):
    pieces, whole = refs[:5], refs[5]
    hidden = widths[0]
    step = hidden // 2
    for start in range(0, hidden, step):
        columns = slice(start, start + step)
        whole[:, columns] = (dot_tn(normed[...], keep[:, columns]) + dot_tn(normed_far[...], got[:, columns])).astype(LOW)
    whole[:, hidden:] = (dot_tn(mixed[...], keep[:, hidden:]) + dot_tn(mixed_far[...], got[:, hidden:])).astype(LOW)
    cut(whole, pieces, lay, index_ref)


def join_kernel(count, index_ref, *refs):
    backs, (d_qkv, send_ref) = refs[: 3 * count], refs[3 * count :]
    core = index_ref[1]
    model = d_qkv.shape[1] // 3
    at = 0
    for number in range(count):
        d_query, own, got = backs[3 * number : 3 * number + 3]
        length, width = d_query.shape
        total = (own[...].astype(FULL) + got[...].astype(FULL)).astype(LOW)
        d_qkv[:, at : at + width] = d_query[...]
        d_qkv[:, model + at : model + at + width] = total[:length, :]
        d_qkv[:, 2 * model + at : 2 * model + at + width] = total[length:, :]
        at += width
    half = model // 2
    for part in range(3):
        start = pl.multiple_of(part * model + (1 - core) * half, LANES)
        send_ref[:, part * half : (part + 1) * half] = d_qkv[:, pl.ds(start, half)]


def last_kernel(index_ref, tokens, small, weights, d_middle, others, d_qkv, grad_ref, sums):
    model = tokens.shape[1]
    d_normed = dot_nt(d_qkv[...], weights[:, : 3 * model])
    hat, scale = normalised(tokens[...].astype(FULL))
    grad_ref[...] = d_middle[...] + normalised_back(d_normed * small[0:1, :], hat, scale)
    sums[...] = others[...]
    sums[0:1, :] = column_sum(d_normed * hat)
    sums[1:2, :] = column_sum(d_normed)
    sums[2:3, :] = column_sum(d_qkv[:, :model])
    sums[3:4, :] = column_sum(d_qkv[:, 2 * model :])


def qkv_grad_kernel(lay, index_ref, normed, normed_far, d_qkv, d_qkv_far, sums, *refs):
    pieces, (whole, tall) = refs[:5], refs[5:]
    core = index_ref[1]
    model = normed.shape[1]
    half = model // 2
    for part in range(3):
        columns = slice(part * half, (part + 1) * half)
        own = d_qkv[:, pl.ds(pl.multiple_of(part * model + core * half, LANES), half)]
        whole[:, columns] = (dot_tn(normed[...], own) + dot_tn(normed_far[...], d_qkv_far[:, columns])).astype(LOW)
    tall[...] = jnp.zeros_like(tall)
    tall[0 : sums.shape[0], :] = sums[...]
    whole[:, 3 * half :] = tall[...].T.astype(LOW)
    cut(whole, pieces, lay, index_ref)


def head_lanes(head):
    lanes = lax.broadcasted_iota(jnp.int32, (1, 2 * HEAD_DIM), 1)
    return (lanes < HEAD_DIM) if head == 0 else (lanes >= HEAD_DIM)


def at_or_before(block):
    query_at = lax.broadcasted_iota(jnp.int32, (block, block), 0)
    key_at = lax.broadcasted_iota(jnp.int32, (block, block), 1)
    return query_at >= key_at


def softmax_parts(scores, values):
    top = functools.reduce(jnp.maximum, [jnp.max(s, axis=1, keepdims=True) for s in scores])
    weights = [jnp.exp(s - top) for s in scores]
    total = sum(jnp.sum(w, axis=1, keepdims=True) for w in weights)
    out = sum(dot_nn(w.astype(jnp.bfloat16), v) for w, v in zip(weights, values))
    return top, total, out


def merge_parts(left, right):
    top = jnp.maximum(left[0], right[0])
    left_scale, right_scale = jnp.exp(left[0] - top), jnp.exp(right[0] - top)
    return (
        top,
        left[1] * left_scale + right[1] * right_scale,
        left[2] * left_scale + right[2] * right_scale,
    )


def attend_kernel(n_ctx, early_ref, query_ref, own_key, own_value, far_key, far_value, out_ref, exact_ref, lse_ref):
    block = query_ref.shape[0] // 2
    causal = at_or_before(block)
    results = []
    for head in (0, 1):
        lanes = head_lanes(head)
        zero = jnp.zeros((), jnp.bfloat16)

        def rows_of(start):
            return jnp.where(lanes, query_ref[pl.ds(start, block), :] * HEAD_DIM**-0.5, zero)

        def keys_of(start, far=False):
            return (far_key if far else own_key)[pl.ds(start, block), :]

        def values_of(start, far=False):
            return (far_value if far else own_value)[pl.ds(start, block), :]

        query_low, query_high = rows_of(0), rows_of(block)
        low = softmax_parts([jnp.where(causal, dot_nt(query_low, keys_of(0)), NEG_FILL)], [values_of(0)])
        seen = [(0, False)] + [(2 * other * block, True) for other in range(n_ctx - 1)]
        high = softmax_parts(
            [jnp.where(causal, dot_nt(query_high, keys_of(block)), NEG_FILL)]
            + [dot_nt(query_high, keys_of(*at)) for at in seen],
            [values_of(block)] + [values_of(*at) for at in seen],
        )
        for other in range(n_ctx - 1):
            early = early_ref[other + 1]
            query_at = pl.multiple_of((1 - early) * block, block)
            key_at = pl.multiple_of((2 * other + 1 - early) * block, block)
            top, total, out = softmax_parts([dot_nt(rows_of(query_at), keys_of(key_at, True))], [values_of(key_at, True)])
            low = merge_parts(low, (jnp.where(early == 1, top, NEG_FILL), total, out))
            high = merge_parts(high, (jnp.where(early == 1, NEG_FILL, top), total, out))
        results.append((low, high))
    lanes = head_lanes(0)
    for half in (0, 1):
        (top_a, total_a, out_a), (top_b, total_b, out_b) = results[0][half], results[1][half]
        rows = pl.ds(half * block, block)
        out = jnp.where(lanes, out_a / total_a, out_b / total_b)
        exact_ref[rows, :] = out
        out_ref[rows, :] = out.astype(out_ref.dtype)
        lse_ref[rows, :] = jnp.where(lanes, top_a + jnp.log(total_a), top_b + jnp.log(total_b))


def attend_back_kernel(
    n_ctx,
    early_ref,
    query_ref,
    own_key,
    own_value,
    far_key,
    far_value,
    dmix_ref,
    out_ref,
    lse_ref,
    dq_ref,
    own_ref,
    far_ref,
    dq_sum,
    dk_own,
    dv_own,
    dk_far,
    dv_far,
):
    block = query_ref.shape[0] // 2
    causal = at_or_before(block)
    zero = jnp.zeros((), jnp.bfloat16)
    for total in (dq_sum, dk_own, dv_own, dk_far, dv_far):
        total[...] = jnp.zeros_like(total)
    for head in (0, 1):
        lanes = head_lanes(head)

        def pair(query_at, key_at, mask=None, far=False):
            key_ref, value_ref, dk_sum, dv_sum = (
                (far_key, far_value, dk_far, dv_far) if far else (own_key, own_value, dk_own, dv_own)
            )
            query_rows, key_rows = pl.ds(query_at, block), pl.ds(key_at, block)
            query = jnp.where(lanes, query_ref[query_rows, :] * HEAD_DIM**-0.5, zero)
            dmix = jnp.where(lanes, dmix_ref[query_rows, :], zero)
            keys = key_ref[key_rows, :]
            product = dmix.astype(jnp.float32) * out_ref[query_rows, :]
            delta = jnp.sum(product, axis=1, keepdims=True)
            lse = lse_ref[query_rows, head * HEAD_DIM : head * HEAD_DIM + 1]
            chances = jnp.exp(dot_nt(query, keys) - lse)
            if mask is not None:
                chances = jnp.where(mask, chances, 0.0)
            d_scores = (chances * (dot_nt(dmix, value_ref[key_rows, :]) - delta)).astype(jnp.bfloat16)
            dq_sum[query_rows, :] += dot_nn(d_scores, jnp.where(lanes, keys, zero))
            dk_sum[key_rows, :] += dot_tn(d_scores, query)
            dv_sum[key_rows, :] += dot_tn(chances.astype(jnp.bfloat16), dmix)

        pair(0, 0, causal)
        pair(block, block, causal)
        pair(block, 0)
        for other in range(n_ctx - 1):
            pair(block, 2 * other * block, far=True)
            early = early_ref[other + 1]
            pair(
                pl.multiple_of((1 - early) * block, block),
                pl.multiple_of((2 * other + 1 - early) * block, block),
                far=True,
            )
    dq_ref[...] = (dq_sum[...] * HEAD_DIM**-0.5).astype(dq_ref.dtype)
    for target, first, second in ((own_ref, dk_own, dv_own), (far_ref, dk_far, dv_far)):
        rows = first.shape[0]
        target[:rows, :] = first[...].astype(target.dtype)
        target[rows:, :] = second[...].astype(target.dtype)


def pair_spec(rows, start=0, part=0):
    return pl.BlockSpec((rows, 2 * HEAD_DIM), lambda pair: (part, start + pair))


def context_of(context, start=0):
    operands = tuple(member for member in context for part in (0, 1))
    specs = [pair_spec(member.shape[0] // 2, start, part) for member in context for part in (0, 1)]
    return operands, specs


def attend(early, queries, context, n_ctx):
    length, width = queries.shape
    operands, specs = context_of(context)
    return pl.pallas_call(
        functools.partial(attend_kernel, n_ctx),
        grid=(width // (2 * HEAD_DIM),),
        out_shape=[shaped(length, width), shaped(length, width, FULL), shaped(length, width, FULL)],
        in_specs=[pl.BlockSpec(memory_space=pltpu.SMEM), pair_spec(length)] + specs,
        out_specs=[pair_spec(length)] * 3,
        compiler_params=pltpu.CompilerParams(vmem_limit_bytes=VMEM_BYTES),
        cost_estimate=pl.CostEstimate(
            flops=16 * n_ctx * length * length * width, bytes_accessed=14 * length * width, transcendentals=0
        ),
    )(early, queries, *operands)


def attend_back(early, queries, context, dmix, out, lse, n_ctx, start, stop):
    length = queries.shape[0]
    others = context[1].shape[0] // 2
    span = (stop - start) * 2 * HEAD_DIM
    operands, specs = context_of(context, start)
    rest = (dmix, out, lse)
    heights = [length, 2 * length, 2 * others]
    sums = [length, length, length, others, others]
    return pl.pallas_call(
        functools.partial(attend_back_kernel, n_ctx),
        grid=(stop - start,),
        out_shape=[shaped(height, span) for height in heights],
        in_specs=[pl.BlockSpec(memory_space=pltpu.SMEM), pair_spec(length, start)]
        + specs
        + [pair_spec(length, start)] * 3,
        out_specs=[pair_spec(height) for height in heights],
        scratch_shapes=[pltpu.VMEM((height, 2 * HEAD_DIM), FULL) for height in sums],
        compiler_params=pltpu.CompilerParams(vmem_limit_bytes=VMEM_BYTES),
        cost_estimate=pl.CostEstimate(
            flops=40 * n_ctx * length * length * span, bytes_accessed=20 * length * span, transcendentals=0
        ),
    )(early, queries, *operands, *rest)


def gather_ctx(both, n_ctx, ctx_index):
    if n_ctx == 2:
        return swap_core(both, n_ctx)
    length = both.shape[0] // 2
    whole = lax.all_gather(both.reshape(2, length, -1), "ctx", axis=1, tiled=True)
    whole = jnp.roll(whole, -ctx_index * length, axis=1)[:, length:]
    return whole.reshape(-1, both.shape[1])


def scatter_ctx(own, far, n_ctx, ctx_index):
    if n_ctx == 2:
        return own, swap_core(far, n_ctx)
    length, width = own.shape[0] // 2, own.shape[1]
    whole = jnp.concatenate([own.reshape(2, length, width), far.reshape(2, -1, width)], axis=1)
    whole = jnp.roll(whole, ctx_index * length, axis=1)
    total = lax.psum_scatter(whole, "ctx", scatter_dimension=1, tiled=True)
    return total.reshape(own.shape), jnp.zeros_like(own)


def body(
    tokens,
    pair_order,
    gain_one,
    bias_one,
    w_qkv,
    bias_q,
    bias_v,
    w_out,
    bias_out,
    gain_two,
    bias_two,
    w_fc,
    bias_fc,
    w_proj,
    bias_proj,
    cotangent,
):
    model = tokens.shape[-1]
    length = tokens.shape[2]
    fsdp, n_ctx = lax.axis_size("fsdp"), lax.axis_size("ctx")
    ctx_index = lax.axis_index("ctx")
    core = ctx_index & 1
    chip = lax.axis_index("fsdp")
    lay = Layout(fsdp, n_ctx, gain_one.shape[0])
    share = (chip & ((1 << lay.merge) - 1)) * n_ctx + ctx_index
    where = jnp.stack([chip >> lay.merge, core]).astype(jnp.int32)
    rows, depth = lay.rows, lay.depth
    tokens_in = tokens.reshape(length, model)
    cotangent_in = cotangent.reshape(length, model)
    vectors = [gain_one, bias_one, bias_q, bias_v, bias_out, gain_two, bias_two, bias_proj]
    bias_rows = lay.merged(bias_fc).reshape(-1, rows)
    blocks = bias_rows.shape[0]
    small_count = SMALL + blocks
    small_rows = jnp.concatenate([lay.merged(jnp.stack(vectors, axis=1)), bias_rows.T], axis=1)
    small_rows = jnp.pad(small_rows, ((0, 0), (0, 2 * LANES - small_count)))
    hidden = w_fc.shape[1]
    widths_one = (model // 2,) * 3 + (LANES,)
    widths_two = (hidden // 2, model // 2)
    qkv_shard = lay.merged(w_qkv)
    half_one = half_of([qkv_shard[:, i * model : (i + 1) * model] for i in range(3)] + [small_rows], core)
    half_two = half_of([lay.merged(w_fc), lay.merged(w_out)], core)
    half_three = half_of([lay.merged(w_proj)], core)
    proj_rows = half_three.shape[1]

    bar = lax.optimization_barrier
    first_steps, last_steps = far_steps(lay)
    kernel_of = functools.partial

    far_one = [half_one] + gather_far(half_one, lay, range(1, lay.depth))
    cotangent_far = swap_core(cotangent_in, n_ctx)
    far_one, half_two, cotangent_far = bar((far_one, half_two, cotangent_far))
    near_one = gather_near(far_one, lay)
    far_two = [half_two] + gather_far(half_two, lay, first_steps)
    core_one = core_of(near_one[:1], lay)
    near_one, far_two, half_two, core_one = bar((near_one, far_two, half_two, core_one))
    corner_one = gather_corner(near_one, lay)
    core_one = core_one + core_of(near_one[1:], lay)
    far_two = far_two + gather_far(half_two, lay, last_steps)
    corner_one, far_two, core_one, half_three = bar((corner_one, far_two, core_one, half_three))
    pieces_one = near_one + corner_one + core_one + core_of(corner_one, lay)
    near_two = gather_near(far_two, lay)
    core_two = core_of(near_two[:1], lay)
    far_three = [half_three] + gather_far(half_three, lay, first_steps)
    normed_one, queries, both, whole_one, small = call(
        kernel_of(first_kernel, lay, widths_one),
        [shaped(length, model)] * 2
        + [shaped(2 * length, model), shaped(model, 2 * sum(widths_one)), shaped(16, model, FULL)],
        where,
        (tokens_in,) + pieces_one,
        flops=6 * length * model * model,
    )
    both, near_two, core_two, far_three, half_three = bar((both, near_two, core_two, far_three, half_three))
    context = (both, gather_ctx(both, n_ctx, ctx_index))
    corner_two = gather_corner(near_two, lay)
    core_two = core_two + core_of(near_two[1:], lay)
    far_three = far_three + gather_far(half_three, lay, last_steps)
    pairs = jnp.roll(pair_order[0], -ctx_index)
    early = (pairs < pairs[0]).astype(jnp.int32)
    mixed, exact, lse = attend(early, queries, context, n_ctx)
    mixed, corner_two, core_two, far_three = bar((mixed, corner_two, core_two, far_three))
    pieces_two = near_two + corner_two + core_two + core_of(corner_two, lay)
    near_three = gather_near(far_three, lay)
    core_three = core_of(near_three[:1], lay)
    mixed_far = swap_core(mixed, n_ctx)
    fc_bias = jnp.moveaxis(small[SMALL:small_count].reshape(blocks, lay.chips, rows), 0, 1).reshape(1, hidden)
    middle, normed_two, active, slope = call(
        kernel_of(hidden_kernel, lay, widths_two),
        [shaped(length, model, FULL), shaped(length, model), shaped(length, hidden), shaped(length, hidden)],
        where,
        (mixed, tokens_in, small, fc_bias) + pieces_two,
        [pltpu.VMEM((model, 2 * sum(widths_two)), LOW)],
        flops=2 * length * model * (model + hidden),
    )
    active, normed_two, near_three, core_three, mixed_far = bar((active, normed_two, near_three, core_three, mixed_far))
    active_far = swap_core(active, n_ctx)
    corner_three = gather_corner(near_three, lay)
    core_three = core_three + core_of(near_three[1:], lay)
    *share_three, sum_cotangent = call(
        kernel_of(proj_grad_kernel, lay),
        piece_shapes(lay, proj_rows, model // 2) + [shaped(1, model, FULL)],
        where,
        (active, active_far, cotangent_in, cotangent_far),
        [pltpu.VMEM((hidden, model // 2), LOW)],
        flops=2 * length * model * hidden,
    )
    share_three, corner_three, core_three = bar((share_three, corner_three, core_three))
    pieces_three = near_three + corner_three + core_three + core_of(corner_three, lay)
    share_three = scatter_corner(share_three, lay)
    normed_one_far, normed_two_far = swap_core(normed_one, n_ctx), swap_core(normed_two, n_ctx)
    out_rows, d_both, d_both_send, d_middle, d_mixed, sums, hidden_sums = call(
        kernel_of(middle_kernel, lay, widths_two),
        [
            shaped(length, model),
            shaped(length, sum(widths_two)),
            shaped(length, sum(widths_two)),
            shaped(length, model, FULL),
            shaped(length, model),
            shaped(8, model, FULL),
            shaped(1, hidden, FULL),
        ],
        where,
        (cotangent_in,) + pieces_three + (slope,) + pieces_two + (middle, small, active),
        [
            pltpu.VMEM((hidden, model), LOW),
            pltpu.VMEM((model, 2 * sum(widths_two)), LOW),
            pltpu.VMEM((length, hidden), LOW),
            pltpu.VMEM((length, model), LOW),
        ],
        flops=6 * length * model * hidden,
    )
    d_mixed, d_both_send, share_three, normed_one_far, normed_two_far = bar(
        (d_mixed, d_both_send, share_three, normed_one_far, normed_two_far)
    )

    def back(start, stop):
        return attend_back(early, queries, context, d_mixed, exact, lse, n_ctx, start, stop)

    def joined(parts):
        return (parts[0],) + scatter_ctx(parts[1], parts[2], n_ctx, ctx_index)

    pair_count = model // (2 * HEAD_DIM)
    cuts = [pair_count * i // 3 for i in range(4)]
    own_three, low_three, high_three = scatter_near_sums(share_three, lay)
    low_three = scatter_near(low_three, lay)
    d_both_far = swap_core(d_both_send, n_ctx)
    back_one = back(cuts[0], cuts[1])
    back_one, low_three, high_three, d_both_far = bar((back_one, low_three, high_three, d_both_far))
    high_three = scatter_near(high_three, lay)
    back_one = joined(back_one)
    share_two = call(
        kernel_of(hidden_grad_kernel, lay, widths_two),
        piece_shapes(lay, rows, sum(widths_two)),
        where,
        (normed_two, normed_two_far, mixed, mixed_far, d_both, d_both_far),
        [pltpu.VMEM((model, sum(widths_two)), LOW)],
        flops=2 * length * model * (model + hidden),
    )
    d_mixed, share_two, back_one, high_three = bar((d_mixed, share_two, back_one, high_three))
    share_two = scatter_corner(share_two, lay)
    parts_three = scatter_far_parts(own_three, low_three, high_three, lay)
    total_three = scatter_far(parts_three, lay, range(1, lay.depth))
    back_two = back(cuts[1], cuts[2])
    d_mixed, share_two, back_two, total_three = bar((d_mixed, share_two, back_two, total_three))
    own_two, low_two, high_two = scatter_near_sums(share_two, lay)
    low_two = scatter_near(low_two, lay)
    back_two = joined(back_two)
    back_three = back(cuts[2], cuts[3])
    back_two, back_three, low_two, high_two = bar((back_two, back_three, low_two, high_two))
    high_two = scatter_near(high_two, lay)
    backs = (back_one, back_two, joined(back_three))
    d_qkv, d_qkv_send = call(
        kernel_of(join_kernel, len(backs)),
        [shaped(length, 3 * model), shaped(length, 3 * model // 2)],
        where,
        sum(backs, ()),
    )
    d_qkv_far = swap_core(d_qkv_send, n_ctx)
    others = jnp.concatenate(
        [
            jnp.zeros((4, model), FULL),
            sums[2:3],
            sums[0:2],
            sum_cotangent,
            jnp.moveaxis(hidden_sums.reshape(lay.chips, lay.shares, blocks, rows // lay.shares), 2, 0).reshape(blocks, model),
            jnp.zeros((16 - small_count, model), FULL),
        ]
    )
    grad_rows, all_sums = call(
        last_kernel,
        [shaped(length, model, FULL), shaped(16, model, FULL)],
        where,
        (tokens_in, small, whole_one, d_middle, others, d_qkv),
        flops=6 * length * model * model,
    )
    all_sums, high_two, d_qkv_far = bar((all_sums, high_two, d_qkv_far))
    parts_two = scatter_far_parts(own_two, low_two, high_two, lay)
    total_two = scatter_far(parts_two, lay, first_steps)
    share_one = call(
        kernel_of(qkv_grad_kernel, lay),
        piece_shapes(lay, rows, sum(widths_one)),
        where,
        (normed_one, normed_one_far, d_qkv, d_qkv_far, all_sums),
        [pltpu.VMEM((model, sum(widths_one)), LOW), pltpu.VMEM((LANES, model), FULL)],
        flops=6 * length * model * model,
    )
    share_one, total_two, parts_two = bar((share_one, total_two, parts_two))
    share_one = scatter_corner(share_one, lay)
    total_two = parts_two[:1] + total_two + scatter_far(parts_two, lay, last_steps)
    share_one, total_two = bar((share_one, total_two))
    own_one, low_one, high_one = scatter_near_sums(share_one, lay)
    low_one, high_one = scatter_near(low_one, lay), scatter_near(high_one, lay)
    parts_one = scatter_far_parts(own_one, low_one, high_one, lay)
    total_one = parts_one[:1] + scatter_far(parts_one, lay, range(1, lay.depth))
    ones = share_rows(scatter_end(total_one, lay), lay, share)
    twos = share_rows(scatter_end(total_two, lay), lay, share)
    threes = share_rows(scatter_end(parts_three[:1] + total_three, lay), lay, share)
    half = model // 2
    grad_qkv = jnp.concatenate(
        [side[:, i * half : (i + 1) * half] for i in range(3) for side in ones], axis=1
    )
    grad_fc = jnp.concatenate([side[:, : hidden // 2] for side in twos], axis=1)
    grad_out = jnp.concatenate([side[:, hidden // 2 :] for side in twos], axis=1)
    grad_proj = jnp.concatenate(threes, axis=1)
    small_share = sum(side[:, 3 * half : 3 * half + small_count] for side in ones).T
    names = ("gain_one", "bias_one", "bias_q", "bias_v", "bias_out", "gain_two", "bias_two", "bias_proj")
    small_grads = dict(zip(names, small_share))
    return (
        out_rows.reshape(tokens.shape),
        grad_rows.reshape(tokens.shape),
        small_grads["gain_one"],
        small_grads["bias_one"],
        grad_qkv,
        small_grads["bias_q"],
        small_grads["bias_v"],
        grad_out,
        small_grads["bias_out"],
        small_grads["gain_two"],
        small_grads["bias_two"],
        grad_fc,
        small_share[SMALL:].reshape(-1),
        grad_proj,
        small_grads["bias_proj"],
    )


def solution(mesh):
    placed = (
        P("fsdp", "ctx", None, None),
        P("fsdp", None),
        P("fsdp"),
        P("fsdp"),
        P("fsdp", None),
        P("fsdp"),
        P("fsdp"),
        P("fsdp", None),
        P("fsdp"),
        P("fsdp"),
        P("fsdp"),
        P("fsdp", None),
        P("fsdp"),
        P("fsdp", None),
        P("fsdp"),
        P("fsdp", "ctx", None, None),
    )
    return jax.shard_map(
        body,
        mesh=mesh,
        in_specs=placed,
        out_specs=(
            P("fsdp", "ctx", None, None),
            P("fsdp", "ctx", None, None),
            P(("fsdp", "ctx")),
            P(("fsdp", "ctx")),
            P(("fsdp", "ctx"), None),
            P(("fsdp", "ctx")),
            P(("fsdp", "ctx")),
            P(("fsdp", "ctx"), None),
            P(("fsdp", "ctx")),
            P(("fsdp", "ctx")),
            P(("fsdp", "ctx")),
            P(("fsdp", "ctx"), None),
            P(("fsdp", "ctx")),
            P(("fsdp", "ctx"), None),
            P(("fsdp", "ctx")),
        ),
        check_vma=False,
    )
```

```python
import functools

import jax
import jax.numpy as jnp
from jax import lax
from jax.experimental import pallas as pl
from jax.experimental.pallas import tpu as pltpu
from jax.sharding import PartitionSpec as P

HEAD_DIM = 64
LANES = 128
EPSILON = 1e-05
NEG_FILL = -1e30
VMEM_BYTES = 56 * 1024 * 1024
LOW = jnp.bfloat16
FULL = jnp.float32
SMALL = 8
GELU_IN = 0.7978845608028654
GELU_CUBE = 0.044715


def dot_nt(left, right):
    return lax.dot_general(left, right, (((1,), (1,)), ((), ())), preferred_element_type=jnp.float32)


def dot_nn(left, right):
    return lax.dot_general(left, right, (((1,), (0,)), ((), ())), preferred_element_type=jnp.float32)


def dot_tn(left, right):
    return lax.dot_general(left, right, (((0,), (0,)), ((), ())), preferred_element_type=jnp.float32)


def swap_chip(value, count, mask):
    return lax.ppermute(value, "fsdp", [(i, i ^ mask) for i in range(count)])


def swap_core(value, count):
    return lax.ppermute(value, "ctx", [(i, i ^ 1) for i in range(count)])


def after(values, others):
    return lax.optimization_barrier((values, others))[0]


class Layout:
    def __init__(self, fsdp, n_ctx, rows):
        self.fsdp, self.n_ctx = fsdp, n_ctx
        self.merge = 0
        while (rows << self.merge) % 16:
            self.merge += 1
        self.rows = rows << self.merge
        self.chips = fsdp >> self.merge
        self.depth = self.chips // 4
        self.shares = n_ctx << self.merge

    def swap(self, value, offset):
        return swap_chip(value, self.fsdp, offset << self.merge)

    def merged(self, shard):
        for bit in range(self.merge):
            other = swap_chip(shard, self.fsdp, 1 << bit)
            first = ((lax.axis_index("fsdp") >> bit) & 1) == 0
            shard = jnp.concatenate([jnp.where(first, shard, other), jnp.where(first, other, shard)], axis=0)
        return shard


def half_of(shards, core):
    halves = [
        lax.dynamic_slice_in_dim(shard, core * (shard.shape[1] // 2), shard.shape[1] // 2, 1) for shard in shards
    ]
    return jnp.concatenate(halves, axis=1)[None]


def far_steps(lay):
    return range(1, lay.depth - 1), range(lay.depth - 1, lay.depth)


def gather_far(own, lay, steps):
    return [lay.swap(own, 4 * j) for j in steps]


def gather_near(far, lay):
    held = jnp.concatenate(far, axis=0)
    return held, lay.swap(held, 1), lay.swap(held, 2)


def gather_corner(near, lay):
    middle = lay.depth // 2
    return lay.swap(near[2][:middle], 1), lay.swap(near[1][middle:], 2)


def core_of(pieces, lay):
    return tuple(swap_core(piece, lay.n_ctx) for piece in pieces)


def piece_offsets(lay):
    middle = lay.depth // 2
    whole = [[m ^ (4 * j) for j in range(lay.depth)] for m in range(4)]
    return [whole[0], whole[1], whole[2], whole[3][:middle], whole[3][middle:]]


def windows(lay, index_ref, rows, widths, sides):
    chip, core = index_ref[0], index_ref[1]
    for other in range(sides):
        side = (1 - core) if other else core
        for number, offsets in enumerate(piece_offsets(lay)):
            for place, offset in enumerate(offsets):
                row = pl.ds(pl.multiple_of((chip ^ offset) * rows, 16), rows)
                at = 0
                for width in widths:
                    column = pl.ds(pl.multiple_of(2 * at + side * width, LANES), width)
                    yield 5 * other + number, place, slice(at, at + width), row, column
                    at += width


def fill(whole, pieces, lay, index_ref, widths):
    for number, place, columns, row, column in windows(lay, index_ref, pieces[0].shape[1], widths, 2):
        whole[row, column] = pieces[number][place, :, columns]


def cut(whole, pieces, lay, index_ref):
    rows = pieces[0].shape[1]
    chip = index_ref[0]
    for number, offsets in enumerate(piece_offsets(lay)):
        for place, offset in enumerate(offsets):
            pieces[number][place] = whole[pl.ds(pl.multiple_of((chip ^ offset) * rows, 16), rows), :]


def piece_shapes(lay, rows, half):
    return [jax.ShapeDtypeStruct((len(offsets), rows, half), LOW) for offsets in piece_offsets(lay)]


def low_sum(*members):
    return sum(member.astype(FULL) for member in members).astype(LOW)


def scatter_corner(sums, lay):
    return tuple(sums[:3]) + (lay.swap(sums[3], 1), lay.swap(sums[4], 2))


def scatter_near_sums(sums, lay):
    middle = lay.depth // 2
    own, one, two, to_two, to_one = sums
    return own, (one[:middle], low_sum(two[:middle], to_two)), (low_sum(one[middle:], to_one), two[middle:])


def scatter_near(pair, lay):
    return lay.swap(pair[0], 1), lay.swap(pair[1], 2)


def scatter_far_parts(own, low, high, lay):
    middle = lay.depth // 2
    return [
        low_sum(own[j], *(member[j if j < middle else j - middle] for member in (low if j < middle else high)))
        for j in range(lay.depth)
    ]


def scatter_far(parts, lay, steps):
    return [lay.swap(parts[j], 4 * j) for j in steps]


def scatter_end(parts, lay):
    total = sum(part.astype(FULL) for part in parts)
    if lay.n_ctx > 2:
        groups = [list(range(0, lay.n_ctx, 2)), list(range(1, lay.n_ctx, 2))]
        total = lax.psum(total, "ctx", axis_index_groups=groups)
    for bit in range(lay.merge):
        total = total + swap_chip(total, lay.fsdp, 1 << bit)
    return total


def share_rows(total, lay, share):
    rows = total.shape[0] // lay.shares
    mine = lax.dynamic_slice_in_dim(total, share * rows, rows, 0)
    theirs = swap_core(lax.dynamic_slice_in_dim(total, (share ^ 1) * rows, rows, 0), lay.n_ctx)
    first = (share & 1) == 0
    return jnp.where(first, mine, theirs), jnp.where(first, theirs, mine)


def call(kernel, out_shape, scalars, arrays, scratch=(), flops=0):
    moved = sum(member.size * member.dtype.itemsize for member in list(arrays) + list(out_shape))
    return pl.pallas_call(
        kernel,
        out_shape=out_shape,
        in_specs=[pl.BlockSpec(memory_space=pltpu.SMEM)] + [pl.BlockSpec(memory_space=pltpu.VMEM)] * len(arrays),
        out_specs=[pl.BlockSpec(memory_space=pltpu.VMEM)] * len(out_shape),
        scratch_shapes=list(scratch),
        compiler_params=pltpu.CompilerParams(vmem_limit_bytes=VMEM_BYTES),
        cost_estimate=pl.CostEstimate(flops=3 * flops, bytes_accessed=moved, transcendentals=0),
    )(scalars, *arrays)


def shaped(rows, columns, dtype=LOW):
    return jax.ShapeDtypeStruct((rows, columns), dtype)


def normalised(values):
    average = jnp.mean(values, axis=-1, keepdims=True)
    centred = values - average
    scale = lax.rsqrt(jnp.mean(centred * centred, axis=-1, keepdims=True) + EPSILON)
    return centred * scale, scale


def normalised_back(grads, hat, scale):
    return (grads - jnp.mean(grads, axis=-1, keepdims=True) - hat * jnp.mean(grads * hat, axis=-1, keepdims=True)) * scale


def column_sum(values):
    return jnp.sum(values.astype(FULL), axis=0, keepdims=True)


def half_at(ref, side):
    width = ref.shape[1] // 2
    return ref[:, pl.ds(pl.multiple_of(side * width, LANES), width)]


def first_kernel(lay, widths, index_ref, tokens, *refs):
    pieces, (normed_ref, query_ref, both_ref, whole, small_ref) = refs[:10], refs[10:]
    model = tokens.shape[1]
    fill(whole, pieces, lay, index_ref, widths)
    small = whole[:, 3 * model : 3 * model + LANES].astype(FULL).T
    small_ref[...] = small[: small_ref.shape[0], :]
    hat, scale = normalised(tokens[...].astype(FULL))
    normed = (hat * small_ref[0:1, :] + small_ref[1:2, :]).astype(LOW)
    normed_ref[...] = normed
    length = normed.shape[0]
    both_ref[:length, :] = dot_nn(normed, whole[:, model : 2 * model]).astype(LOW)
    both_ref[length:, :] = (dot_nn(normed, whole[:, 2 * model : 3 * model]) + small_ref[3:4, :]).astype(LOW)
    query_ref[...] = (dot_nn(normed, whole[:, :model]) + small_ref[2:3, :]).astype(LOW)


def hidden_kernel(lay, widths, index_ref, mixed, tokens, small, fc_bias, *refs):
    pieces, (middle_ref, normed_ref, active_ref, slope_ref, whole) = refs[:10], refs[10:]
    model = tokens.shape[1]
    hidden = active_ref.shape[1]
    fill(whole, pieces, lay, index_ref, widths)
    middle = tokens[...].astype(FULL) + dot_nn(mixed[...], whole[:, hidden:]) + small[4:5, :]
    middle_ref[...] = middle
    hat, scale = normalised(middle)
    normed = (hat * small[5:6, :] + small[6:7, :]).astype(LOW)
    normed_ref[...] = normed
    for start in range(0, hidden, model):
        columns = slice(start, start + model)
        pre = dot_nn(normed, whole[:, columns]) + fc_bias[:, columns]
        square = pre * pre
        part = 0.5 + 0.5 * jnp.tanh(pre * (GELU_IN + GELU_IN * GELU_CUBE * square))
        active = pre * part
        active_ref[:, columns] = active.astype(LOW)
        slope = part + active * (1.0 - part) * (2.0 * GELU_IN + 6.0 * GELU_IN * GELU_CUBE * square)
        slope_ref[:, columns] = slope.astype(LOW)


def proj_grad_kernel(lay, index_ref, active, active_far, cotangent, cotangent_far, *refs):
    pieces, (sum_ref, whole) = refs[:5], refs[5:]
    model = cotangent.shape[1]
    core = index_ref[1]
    sum_ref[...] = column_sum(cotangent[...])
    own, far = half_at(cotangent, core), half_at(cotangent_far, core)
    for start in range(0, active.shape[1], model):
        columns = slice(start, start + model)
        whole[columns, :] = (dot_tn(active[:, columns], own) + dot_tn(active_far[:, columns], far)).astype(LOW)
    cut(whole, pieces, lay, index_ref)


def middle_kernel(lay, widths, index_ref, cotangent, *refs):
    core = index_ref[1]
    proj_pieces, slope, pieces, (middle_ref, small, active), refs = refs[:10], refs[10], refs[11:21], refs[21:24], refs[24:]
    out_ref, keep_ref, send_ref, d_middle_ref, d_mixed_ref, sums_ref, hidden_sums_ref = refs[:7]
    proj, weights, d_pre_all, d_branch_all = refs[7:]
    model = cotangent.shape[1]
    hidden = active.shape[1]
    fill(proj, proj_pieces, lay, index_ref, (model // 2,))
    d_normed = None
    for start in range(0, hidden, model):
        columns = slice(start, start + model)
        d_active = dot_nt(cotangent[...], proj[columns, :])
        d_pre = (d_active * slope[:, columns].astype(FULL)).astype(LOW)
        d_pre_all[:, columns] = d_pre
        hidden_sums_ref[:, columns] = column_sum(d_pre)
        if start == 0:
            fill(weights, pieces, lay, index_ref, widths)
        part = dot_nt(d_pre, weights[:, columns])
        d_normed = part if d_normed is None else d_normed + part
    keep_ref[:, : hidden // 2] = half_at(d_pre_all, core)
    send_ref[:, : hidden // 2] = half_at(d_pre_all, 1 - core)
    hat, scale = normalised(middle_ref[...])
    sums_ref[0:1, :] = column_sum(d_normed * hat)
    sums_ref[1:2, :] = column_sum(d_normed)
    d_middle = cotangent[...].astype(FULL) + normalised_back(d_normed * small[5:6, :], hat, scale)
    d_middle_ref[...] = d_middle
    d_branch = d_middle.astype(LOW)
    d_branch_all[...] = d_branch
    keep_ref[:, hidden // 2 :] = half_at(d_branch_all, core)
    send_ref[:, hidden // 2 :] = half_at(d_branch_all, 1 - core)
    sums_ref[2:3, :] = column_sum(d_branch)
    d_mixed_ref[...] = dot_nt(d_branch, weights[:, hidden:]).astype(LOW)
    out_ref[...] = (middle_ref[...] + dot_nn(active[...], proj[...]) + small[7:8, :]).astype(LOW)


def hidden_grad_kernel(lay, widths, index_ref, normed, normed_far, mixed, mixed_far, keep, got, *refs):
    pieces, whole = refs[:5], refs[5]
    hidden = widths[0]
    step = hidden // 2
    for start in range(0, hidden, step):
        columns = slice(start, start + step)
        whole[:, columns] = (dot_tn(normed[...], keep[:, columns]) + dot_tn(normed_far[...], got[:, columns])).astype(LOW)
    whole[:, hidden:] = (dot_tn(mixed[...], keep[:, hidden:]) + dot_tn(mixed_far[...], got[:, hidden:])).astype(LOW)
    cut(whole, pieces, lay, index_ref)


def join_kernel(count, index_ref, *refs):
    backs, (d_qkv, send_ref) = refs[: 3 * count], refs[3 * count :]
    core = index_ref[1]
    model = d_qkv.shape[1] // 3
    at = 0
    for number in range(count):
        d_query, own, got = backs[3 * number : 3 * number + 3]
        length, width = d_query.shape
        total = (own[...].astype(FULL) + got[...].astype(FULL)).astype(LOW)
        d_qkv[:, at : at + width] = d_query[...]
        d_qkv[:, model + at : model + at + width] = total[:length, :]
        d_qkv[:, 2 * model + at : 2 * model + at + width] = total[length:, :]
        at += width
    half = model // 2
    for part in range(3):
        start = pl.multiple_of(part * model + (1 - core) * half, LANES)
        send_ref[:, part * half : (part + 1) * half] = d_qkv[:, pl.ds(start, half)]


def last_kernel(index_ref, tokens, small, weights, d_middle, others, d_qkv, grad_ref, sums):
    model = tokens.shape[1]
    d_normed = dot_nt(d_qkv[...], weights[:, : 3 * model])
    hat, scale = normalised(tokens[...].astype(FULL))
    grad_ref[...] = d_middle[...] + normalised_back(d_normed * small[0:1, :], hat, scale)
    sums[...] = others[...]
    sums[0:1, :] = column_sum(d_normed * hat)
    sums[1:2, :] = column_sum(d_normed)
    sums[2:3, :] = column_sum(d_qkv[:, :model])
    sums[3:4, :] = column_sum(d_qkv[:, 2 * model :])


def qkv_grad_kernel(lay, index_ref, normed, normed_far, d_qkv, d_qkv_far, sums, *refs):
    pieces, (whole, tall) = refs[:5], refs[5:]
    core = index_ref[1]
    model = normed.shape[1]
    half = model // 2
    for part in range(3):
        columns = slice(part * half, (part + 1) * half)
        own = d_qkv[:, pl.ds(pl.multiple_of(part * model + core * half, LANES), half)]
        whole[:, columns] = (dot_tn(normed[...], own) + dot_tn(normed_far[...], d_qkv_far[:, columns])).astype(LOW)
    tall[...] = jnp.zeros_like(tall)
    tall[0 : sums.shape[0], :] = sums[...]
    whole[:, 3 * half :] = tall[...].T.astype(LOW)
    cut(whole, pieces, lay, index_ref)


def head_lanes(head):
    lanes = lax.broadcasted_iota(jnp.int32, (1, 2 * HEAD_DIM), 1)
    return (lanes < HEAD_DIM) if head == 0 else (lanes >= HEAD_DIM)


def at_or_before(block):
    query_at = lax.broadcasted_iota(jnp.int32, (block, block), 0)
    key_at = lax.broadcasted_iota(jnp.int32, (block, block), 1)
    return query_at >= key_at


def not_after(block):
    key_at = lax.broadcasted_iota(jnp.int32, (block, block), 0)
    query_at = lax.broadcasted_iota(jnp.int32, (block, block), 1)
    return key_at <= query_at


def softmax_parts(scores, values):
    top = functools.reduce(jnp.maximum, [jnp.max(s, axis=0, keepdims=True) for s in scores])
    weights = [jnp.exp(s - top) for s in scores]
    total = sum(jnp.sum(w, axis=0, keepdims=True) for w in weights)
    out = sum(dot_tn(v, w.astype(jnp.bfloat16)) for w, v in zip(weights, values))
    return top, total, out


def merge_parts(left, right):
    top = jnp.maximum(left[0], right[0])
    left_scale, right_scale = jnp.exp(left[0] - top), jnp.exp(right[0] - top)
    return (
        top,
        left[1] * left_scale + right[1] * right_scale,
        left[2] * left_scale + right[2] * right_scale,
    )


def attend_kernel(
    n_ctx, early_ref, query_ref, own_key, own_value, far_key, far_value, out_ref, exact_ref, lse_ref
):
    block = query_ref.shape[0] // 2
    causal = not_after(block)
    results = []
    for head in (0, 1):
        lanes = head_lanes(head)
        zero = jnp.zeros((), jnp.bfloat16)

        def rows_of(start):
            return jnp.where(lanes, query_ref[pl.ds(start, block), :] * HEAD_DIM**-0.5, zero)

        def keys_of(start, far=False):
            return (far_key if far else own_key)[pl.ds(start, block), :]

        def values_of(start, far=False):
            return (far_value if far else own_value)[pl.ds(start, block), :]

        query_low, query_high = rows_of(0), rows_of(block)
        low = softmax_parts([jnp.where(causal, dot_nt(keys_of(0), query_low), NEG_FILL)], [values_of(0)])
        seen = [(0, False)] + [(2 * other * block, True) for other in range(n_ctx - 1)]
        high = softmax_parts(
            [jnp.where(causal, dot_nt(keys_of(block), query_high), NEG_FILL)]
            + [dot_nt(keys_of(*at), query_high) for at in seen],
            [values_of(block)] + [values_of(*at) for at in seen],
        )
        for other in range(n_ctx - 1):
            early = early_ref[other + 1]
            query_at = pl.multiple_of((1 - early) * block, block)
            key_at = pl.multiple_of((2 * other + 1 - early) * block, block)
            top, total, out = softmax_parts(
                [dot_nt(keys_of(key_at, True), rows_of(query_at))], [values_of(key_at, True)]
            )
            low = merge_parts(low, (jnp.where(early == 1, top, NEG_FILL), total, out))
            high = merge_parts(high, (jnp.where(early == 1, NEG_FILL, top), total, out))
        results.append((low, high))
    for half in (0, 1):
        (top_a, total_a, out_a), (top_b, total_b, out_b) = results[0][half], results[1][half]
        rows = slice(half * block, (half + 1) * block)
        out = jnp.concatenate([out_a[:HEAD_DIM] / total_a, out_b[HEAD_DIM:] / total_b], axis=0).T
        exact_ref[rows, :] = out
        out_ref[rows, :] = out.astype(out_ref.dtype)
        lse = [top_a + jnp.log(total_a), top_b + jnp.log(total_b)]
        lse_ref[rows, :] = jnp.concatenate([jnp.broadcast_to(row, (HEAD_DIM, block)) for row in lse], axis=0).T


def attend_back_kernel(
    n_ctx,
    early_ref,
    query_ref,
    own_key,
    own_value,
    far_key,
    far_value,
    dmix_ref,
    out_ref,
    lse_ref,
    dq_ref,
    own_ref,
    far_ref,
    dq_sum,
    dk_own,
    dv_own,
    dk_far,
    dv_far,
):
    block = query_ref.shape[0] // 2
    causal = at_or_before(block)
    zero = jnp.zeros((), jnp.bfloat16)
    for total in (dq_sum, dk_own, dv_own, dk_far, dv_far):
        total[...] = jnp.zeros_like(total)
    for head in (0, 1):
        lanes = head_lanes(head)

        def pair(query_at, key_at, mask=None, far=False):
            key_ref, value_ref, dk_sum, dv_sum = (
                (far_key, far_value, dk_far, dv_far) if far else (own_key, own_value, dk_own, dv_own)
            )
            query_rows, key_rows = pl.ds(query_at, block), pl.ds(key_at, block)
            query = jnp.where(lanes, query_ref[query_rows, :] * HEAD_DIM**-0.5, zero)
            dmix = jnp.where(lanes, dmix_ref[query_rows, :], zero)
            keys = key_ref[key_rows, :]
            product = dmix.astype(jnp.float32) * out_ref[query_rows, :]
            delta = jnp.sum(product, axis=1, keepdims=True)
            lse = lse_ref[query_rows, head * HEAD_DIM : head * HEAD_DIM + 1]
            chances = jnp.exp(dot_nt(query, keys) - lse)
            if mask is not None:
                chances = jnp.where(mask, chances, 0.0)
            d_scores = (chances * (dot_nt(dmix, value_ref[key_rows, :]) - delta)).astype(jnp.bfloat16)
            dq_sum[query_rows, :] += dot_nn(d_scores, jnp.where(lanes, keys, zero))
            dk_sum[key_rows, :] += dot_tn(d_scores, query)
            dv_sum[key_rows, :] += dot_tn(chances.astype(jnp.bfloat16), dmix)

        pair(0, 0, causal)
        pair(block, block, causal)
        pair(block, 0)
        for other in range(n_ctx - 1):
            pair(block, 2 * other * block, far=True)
            early = early_ref[other + 1]
            pair(
                pl.multiple_of((1 - early) * block, block),
                pl.multiple_of((2 * other + 1 - early) * block, block),
                far=True,
            )
    dq_ref[...] = (dq_sum[...] * HEAD_DIM**-0.5).astype(dq_ref.dtype)
    for target, first, second in ((own_ref, dk_own, dv_own), (far_ref, dk_far, dv_far)):
        rows = first.shape[0]
        target[:rows, :] = first[...].astype(target.dtype)
        target[rows:, :] = second[...].astype(target.dtype)


def pair_spec(rows, start=0, part=0):
    return pl.BlockSpec((rows, 2 * HEAD_DIM), lambda pair: (part, start + pair))


def context_of(context, start=0):
    operands = tuple(member for member in context for part in (0, 1))
    specs = [pair_spec(member.shape[0] // 2, start, part) for member in context for part in (0, 1)]
    return operands, specs


def attend(early, queries, context, n_ctx):
    length, width = queries.shape
    operands, specs = context_of(context)
    return pl.pallas_call(
        functools.partial(attend_kernel, n_ctx),
        grid=(width // (2 * HEAD_DIM),),
        out_shape=[shaped(length, width), shaped(length, width, FULL), shaped(length, width, FULL)],
        in_specs=[pl.BlockSpec(memory_space=pltpu.SMEM), pair_spec(length)] + specs,
        out_specs=[pair_spec(length)] * 3,
        compiler_params=pltpu.CompilerParams(vmem_limit_bytes=VMEM_BYTES),
        cost_estimate=pl.CostEstimate(
            flops=16 * n_ctx * length * length * width, bytes_accessed=14 * length * width, transcendentals=0
        ),
    )(early, queries, *operands)


def attend_back(early, queries, context, dmix, out, lse, n_ctx, start, stop):
    length = queries.shape[0]
    others = context[1].shape[0] // 2
    span = (stop - start) * 2 * HEAD_DIM
    operands, specs = context_of(context, start)
    rest = (dmix, out, lse)
    heights = [length, 2 * length, 2 * others]
    sums = [length, length, length, others, others]
    return pl.pallas_call(
        functools.partial(attend_back_kernel, n_ctx),
        grid=(stop - start,),
        out_shape=[shaped(height, span) for height in heights],
        in_specs=[pl.BlockSpec(memory_space=pltpu.SMEM), pair_spec(length, start)]
        + specs
        + [pair_spec(length, start)] * 3,
        out_specs=[pair_spec(height) for height in heights],
        scratch_shapes=[pltpu.VMEM((height, 2 * HEAD_DIM), FULL) for height in sums],
        compiler_params=pltpu.CompilerParams(vmem_limit_bytes=VMEM_BYTES),
        cost_estimate=pl.CostEstimate(
            flops=40 * n_ctx * length * length * span, bytes_accessed=20 * length * span, transcendentals=0
        ),
    )(early, queries, *operands, *rest)


def gather_ctx(both, n_ctx, ctx_index):
    if n_ctx == 2:
        return swap_core(both, n_ctx)
    length = both.shape[0] // 2
    whole = lax.all_gather(both.reshape(2, length, -1), "ctx", axis=1, tiled=True)
    whole = jnp.roll(whole, -ctx_index * length, axis=1)[:, length:]
    return whole.reshape(-1, both.shape[1])


def scatter_ctx(own, far, n_ctx, ctx_index):
    if n_ctx == 2:
        return own, swap_core(far, n_ctx)
    length, width = own.shape[0] // 2, own.shape[1]
    whole = jnp.concatenate([own.reshape(2, length, width), far.reshape(2, -1, width)], axis=1)
    whole = jnp.roll(whole, ctx_index * length, axis=1)
    total = lax.psum_scatter(whole, "ctx", scatter_dimension=1, tiled=True)
    return total.reshape(own.shape), jnp.zeros_like(own)


def body(
    tokens,
    pair_order,
    gain_one,
    bias_one,
    w_qkv,
    bias_q,
    bias_v,
    w_out,
    bias_out,
    gain_two,
    bias_two,
    w_fc,
    bias_fc,
    w_proj,
    bias_proj,
    cotangent,
):
    model = tokens.shape[-1]
    length = tokens.shape[2]
    fsdp, n_ctx = lax.axis_size("fsdp"), lax.axis_size("ctx")
    ctx_index = lax.axis_index("ctx")
    core = ctx_index & 1
    chip = lax.axis_index("fsdp")
    lay = Layout(fsdp, n_ctx, gain_one.shape[0])
    share = (chip & ((1 << lay.merge) - 1)) * n_ctx + ctx_index
    where = jnp.stack([chip >> lay.merge, core]).astype(jnp.int32)
    rows, depth = lay.rows, lay.depth
    tokens_in = tokens.reshape(length, model)
    cotangent_in = cotangent.reshape(length, model)
    vectors = [gain_one, bias_one, bias_q, bias_v, bias_out, gain_two, bias_two, bias_proj]
    bias_rows = lay.merged(bias_fc).reshape(-1, rows)
    blocks = bias_rows.shape[0]
    small_count = SMALL + blocks
    small_rows = jnp.concatenate([lay.merged(jnp.stack(vectors, axis=1)), bias_rows.T], axis=1)
    small_rows = jnp.pad(small_rows, ((0, 0), (0, 2 * LANES - small_count)))
    hidden = w_fc.shape[1]
    widths_one = (model // 2,) * 3 + (LANES,)
    widths_two = (hidden // 2, model // 2)
    qkv_shard = lay.merged(w_qkv)
    half_one = half_of([qkv_shard[:, i * model : (i + 1) * model] for i in range(3)] + [small_rows], core)
    half_two = half_of([lay.merged(w_fc), lay.merged(w_out)], core)
    half_three = half_of([lay.merged(w_proj)], core)
    proj_rows = half_three.shape[1]

    bar = lax.optimization_barrier
    first_steps, last_steps = far_steps(lay)
    kernel_of = functools.partial

    far_one = [half_one] + gather_far(half_one, lay, range(1, lay.depth))
    cotangent_far = swap_core(cotangent_in, n_ctx)
    far_one, half_two, cotangent_far = bar((far_one, half_two, cotangent_far))
    near_one = gather_near(far_one, lay)
    far_two = [half_two] + gather_far(half_two, lay, first_steps)
    core_one = core_of(near_one[:1], lay)
    near_one, far_two, half_two, core_one = bar((near_one, far_two, half_two, core_one))
    corner_one = gather_corner(near_one, lay)
    core_one = core_one + core_of(near_one[1:], lay)
    far_two = far_two + gather_far(half_two, lay, last_steps)
    corner_one, far_two, core_one, half_three = bar((corner_one, far_two, core_one, half_three))
    pieces_one = near_one + corner_one + core_one + core_of(corner_one, lay)
    near_two = gather_near(far_two, lay)
    core_two = core_of(near_two[:1], lay)
    far_three = [half_three] + gather_far(half_three, lay, first_steps)
    normed_one, queries, both, whole_one, small = call(
        kernel_of(first_kernel, lay, widths_one),
        [shaped(length, model)] * 2
        + [shaped(2 * length, model), shaped(model, 2 * sum(widths_one)), shaped(16, model, FULL)],
        where,
        (tokens_in,) + pieces_one,
        flops=6 * length * model * model,
    )
    both, near_two, core_two, far_three, half_three = bar((both, near_two, core_two, far_three, half_three))
    context = (both, gather_ctx(both, n_ctx, ctx_index))
    corner_two = gather_corner(near_two, lay)
    core_two = core_two + core_of(near_two[1:], lay)
    far_three = far_three + gather_far(half_three, lay, last_steps)
    pairs = jnp.roll(pair_order[0], -ctx_index)
    early = (pairs < pairs[0]).astype(jnp.int32)
    mixed, exact, lse = attend(early, queries, context, n_ctx)
    mixed, corner_two, core_two, far_three = bar((mixed, corner_two, core_two, far_three))
    pieces_two = near_two + corner_two + core_two + core_of(corner_two, lay)
    near_three = gather_near(far_three, lay)
    core_three = core_of(near_three[:1], lay)
    mixed_far = swap_core(mixed, n_ctx)
    fc_bias = jnp.moveaxis(small[SMALL:small_count].reshape(blocks, lay.chips, rows), 0, 1).reshape(1, hidden)
    middle, normed_two, active, slope = call(
        kernel_of(hidden_kernel, lay, widths_two),
        [shaped(length, model, FULL), shaped(length, model), shaped(length, hidden), shaped(length, hidden)],
        where,
        (mixed, tokens_in, small, fc_bias) + pieces_two,
        [pltpu.VMEM((model, 2 * sum(widths_two)), LOW)],
        flops=2 * length * model * (model + hidden),
    )
    active, normed_two, near_three, core_three, mixed_far = bar((active, normed_two, near_three, core_three, mixed_far))
    active_far = swap_core(active, n_ctx)
    corner_three = gather_corner(near_three, lay)
    core_three = core_three + core_of(near_three[1:], lay)
    *share_three, sum_cotangent = call(
        kernel_of(proj_grad_kernel, lay),
        piece_shapes(lay, proj_rows, model // 2) + [shaped(1, model, FULL)],
        where,
        (active, active_far, cotangent_in, cotangent_far),
        [pltpu.VMEM((hidden, model // 2), LOW)],
        flops=2 * length * model * hidden,
    )
    share_three, corner_three, core_three = bar((share_three, corner_three, core_three))
    pieces_three = near_three + corner_three + core_three + core_of(corner_three, lay)
    share_three = scatter_corner(share_three, lay)
    normed_one_far, normed_two_far = swap_core(normed_one, n_ctx), swap_core(normed_two, n_ctx)
    out_rows, d_both, d_both_send, d_middle, d_mixed, sums, hidden_sums = call(
        kernel_of(middle_kernel, lay, widths_two),
        [
            shaped(length, model),
            shaped(length, sum(widths_two)),
            shaped(length, sum(widths_two)),
            shaped(length, model, FULL),
            shaped(length, model),
            shaped(8, model, FULL),
            shaped(1, hidden, FULL),
        ],
        where,
        (cotangent_in,) + pieces_three + (slope,) + pieces_two + (middle, small, active),
        [
            pltpu.VMEM((hidden, model), LOW),
            pltpu.VMEM((model, 2 * sum(widths_two)), LOW),
            pltpu.VMEM((length, hidden), LOW),
            pltpu.VMEM((length, model), LOW),
        ],
        flops=6 * length * model * hidden,
    )
    d_mixed, d_both_send, share_three, normed_one_far, normed_two_far = bar(
        (d_mixed, d_both_send, share_three, normed_one_far, normed_two_far)
    )

    def back(start, stop):
        return attend_back(early, queries, context, d_mixed, exact, lse, n_ctx, start, stop)

    def joined(parts):
        return (parts[0],) + scatter_ctx(parts[1], parts[2], n_ctx, ctx_index)

    pair_count = model // (2 * HEAD_DIM)
    cuts = [pair_count * i // 3 for i in range(4)]
    own_three, low_three, high_three = scatter_near_sums(share_three, lay)
    low_three = scatter_near(low_three, lay)
    d_both_far = swap_core(d_both_send, n_ctx)
    back_one = back(cuts[0], cuts[1])
    back_one, low_three, high_three, d_both_far = bar((back_one, low_three, high_three, d_both_far))
    high_three = scatter_near(high_three, lay)
    back_one = joined(back_one)
    share_two = call(
        kernel_of(hidden_grad_kernel, lay, widths_two),
        piece_shapes(lay, rows, sum(widths_two)),
        where,
        (normed_two, normed_two_far, mixed, mixed_far, d_both, d_both_far),
        [pltpu.VMEM((model, sum(widths_two)), LOW)],
        flops=2 * length * model * (model + hidden),
    )
    d_mixed, share_two, back_one, high_three = bar((d_mixed, share_two, back_one, high_three))
    share_two = scatter_corner(share_two, lay)
    parts_three = scatter_far_parts(own_three, low_three, high_three, lay)
    total_three = scatter_far(parts_three, lay, range(1, lay.depth))
    back_two = back(cuts[1], cuts[2])
    d_mixed, share_two, back_two, total_three = bar((d_mixed, share_two, back_two, total_three))
    own_two, low_two, high_two = scatter_near_sums(share_two, lay)
    low_two = scatter_near(low_two, lay)
    back_two = joined(back_two)
    back_three = back(cuts[2], cuts[3])
    back_two, back_three, low_two, high_two = bar((back_two, back_three, low_two, high_two))
    high_two = scatter_near(high_two, lay)
    backs = (back_one, back_two, joined(back_three))
    d_qkv, d_qkv_send = call(
        kernel_of(join_kernel, len(backs)),
        [shaped(length, 3 * model), shaped(length, 3 * model // 2)],
        where,
        sum(backs, ()),
    )
    d_qkv_far = swap_core(d_qkv_send, n_ctx)
    others = jnp.concatenate(
        [
            jnp.zeros((4, model), FULL),
            sums[2:3],
            sums[0:2],
            sum_cotangent,
            jnp.moveaxis(hidden_sums.reshape(lay.chips, lay.shares, blocks, rows // lay.shares), 2, 0).reshape(blocks, model),
            jnp.zeros((16 - small_count, model), FULL),
        ]
    )
    grad_rows, all_sums = call(
        last_kernel,
        [shaped(length, model, FULL), shaped(16, model, FULL)],
        where,
        (tokens_in, small, whole_one, d_middle, others, d_qkv),
        flops=6 * length * model * model,
    )
    all_sums, high_two, d_qkv_far = bar((all_sums, high_two, d_qkv_far))
    parts_two = scatter_far_parts(own_two, low_two, high_two, lay)
    total_two = scatter_far(parts_two, lay, first_steps)
    share_one = call(
        kernel_of(qkv_grad_kernel, lay),
        piece_shapes(lay, rows, sum(widths_one)),
        where,
        (normed_one, normed_one_far, d_qkv, d_qkv_far, all_sums),
        [pltpu.VMEM((model, sum(widths_one)), LOW), pltpu.VMEM((LANES, model), FULL)],
        flops=6 * length * model * model,
    )
    share_one = scatter_corner(share_one, lay)
    share_one, total_two, parts_two = bar((share_one, total_two, parts_two))
    total_two = parts_two[:1] + total_two + scatter_far(parts_two, lay, last_steps)
    own_one, low_one, high_one = scatter_near_sums(share_one, lay)
    low_one, high_one = scatter_near(low_one, lay), scatter_near(high_one, lay)
    parts_one = scatter_far_parts(own_one, low_one, high_one, lay)
    total_one = parts_one[:1] + scatter_far(parts_one, lay, range(1, lay.depth))
    ones = share_rows(scatter_end(total_one, lay), lay, share)
    twos = share_rows(scatter_end(total_two, lay), lay, share)
    threes = share_rows(scatter_end(parts_three[:1] + total_three, lay), lay, share)
    half = model // 2
    grad_qkv = jnp.concatenate(
        [side[:, i * half : (i + 1) * half] for i in range(3) for side in ones], axis=1
    )
    grad_fc = jnp.concatenate([side[:, : hidden // 2] for side in twos], axis=1)
    grad_out = jnp.concatenate([side[:, hidden // 2 :] for side in twos], axis=1)
    grad_proj = jnp.concatenate(threes, axis=1)
    small_share = sum(side[:, 3 * half : 3 * half + small_count] for side in ones).T
    names = ("gain_one", "bias_one", "bias_q", "bias_v", "bias_out", "gain_two", "bias_two", "bias_proj")
    small_grads = dict(zip(names, small_share))
    return (
        out_rows.reshape(tokens.shape),
        grad_rows.reshape(tokens.shape),
        small_grads["gain_one"],
        small_grads["bias_one"],
        grad_qkv,
        small_grads["bias_q"],
        small_grads["bias_v"],
        grad_out,
        small_grads["bias_out"],
        small_grads["gain_two"],
        small_grads["bias_two"],
        grad_fc,
        small_share[SMALL:].reshape(-1),
        grad_proj,
        small_grads["bias_proj"],
    )


def solution(mesh):
    placed = (
        P("fsdp", "ctx", None, None),
        P("fsdp", None),
        P("fsdp"),
        P("fsdp"),
        P("fsdp", None),
        P("fsdp"),
        P("fsdp"),
        P("fsdp", None),
        P("fsdp"),
        P("fsdp"),
        P("fsdp"),
        P("fsdp", None),
        P("fsdp"),
        P("fsdp", None),
        P("fsdp"),
        P("fsdp", "ctx", None, None),
    )
    return jax.shard_map(
        body,
        mesh=mesh,
        in_specs=placed,
        out_specs=(
            P("fsdp", "ctx", None, None),
            P("fsdp", "ctx", None, None),
            P(("fsdp", "ctx")),
            P(("fsdp", "ctx")),
            P(("fsdp", "ctx"), None),
            P(("fsdp", "ctx")),
            P(("fsdp", "ctx")),
            P(("fsdp", "ctx"), None),
            P(("fsdp", "ctx")),
            P(("fsdp", "ctx")),
            P(("fsdp", "ctx")),
            P(("fsdp", "ctx"), None),
            P(("fsdp", "ctx")),
            P(("fsdp", "ctx"), None),
            P(("fsdp", "ctx")),
        ),
        check_vma=False,
    )
```
